32 devices in a mesh: vp: 8 (over z, x), vc: 4 (over y, core).
Axes of the slice: x: 2, y: 2, z: 4, core: 2. Of those that a mesh axis runs over, the one named last changes fastest.
Arguments:
- amplitudes: bfloat16 [64, 102400], P(('vp', 'vc')), may hold values from -6 to 6
- pair_tiles: bfloat16 [8192, 128, 128], P(('vp', 'vc')), may hold values from -0.09375 to 0.09375
- slot_pairs: int32 [8192, 2], P(('vp', 'vc')), may hold values from 0 to 199, as said below
- slot_count: int32 [32], P(('vp', 'vc')), may hold values from 32 to 256, as said below
Outputs:
- ladder: bfloat16 [64, 16384], P('vc', 'vp')
The draws below stay inside these ranges and needn't reach their ends.
Inputs may be any that keep to these rules, and one draw needn't show every extreme that they name: `slot_pairs`: the rows of one device name distinct pairs; column 0 lies in 0 to 15, column 1 in 0 to 199. `slot_count`: every count is 256 divided by 1, 2, 4 or 8; some device has exactly 256.
All inputs are finite; a program needn't handle non-finite values.
Results may differ from the reference program's by a relative error of at most 0.001.
Values may be sent and summed in bfloat16 or wider, within the bound.
A program may use at most 128 MiB of HBM per device.

```python
import jax
import jax.numpy as jnp
from jax import lax

TILE = 128
ABT_DEV = 16
CT_DEV = 200
SLOTS_DEV = 256
PAIRS = 64
CD = 102400
AB = 16384
ALL_SLOTS = 8192
N_VP = 8
N_VC = 4


def draw_slot_pairs(key, part):
    device_keys = jax.random.split(jax.random.fold_in(key, 11), N_VP * N_VC)

    def one_device(device_key):
        shuffled = jax.random.permutation(device_key, ABT_DEV * CT_DEV)[:SLOTS_DEV]
        return jnp.stack([shuffled // CT_DEV, shuffled % CT_DEV], axis=1)
    return jax.vmap(one_device)(device_keys).reshape(N_VP * N_VC * SLOTS_DEV, 2).astype(jnp.int32)


def draw_slot_count(key, part):
    device_total = N_VP * N_VC
    halvings = jax.random.randint(jax.random.fold_in(key, 21), (device_total,), 0, 4)
    counts = jnp.right_shift(jnp.full((device_total,), SLOTS_DEV, jnp.int32), halvings.astype(jnp.int32))
    chosen = jax.random.randint(jax.random.fold_in(key, 22), (), 0, device_total)
    counts = jnp.where(jnp.arange(device_total) == chosen, SLOTS_DEV, counts)
    return counts.astype(jnp.int32)


def levels(own_key, shape, shards, smallest, high):
    gain = 1.0
    for position, blocks in shards:
        draws = jax.random.uniform(jax.random.fold_in(jax.random.fold_in(own_key, 6), position), (blocks,), jnp.float32, smallest / len(shards), high / len(shards))
        gain = gain * jnp.repeat(jnp.exp(draws), shape[position] // blocks).reshape((-1,) + (1,) * (len(shape) - 1 - position))
    return gain


def scatter_about(key, extent, deviation, bound, shards=(), kind=jnp.bfloat16):
    result = jax.random.normal(key, extent, jnp.float32) * deviation
    if len(shards) > 0:
        result = levels(key, extent, shards, -0.22, 0.18) * result
    return jnp.clip(result, min=-bound, max=bound).astype(kind)


def setup_inputs(seed: int = 0) -> dict:
    arg_keys = jax.random.split(jax.random.key(seed), 5)
    return {
        "amplitudes": scatter_about(arg_keys[0], (PAIRS, CD), 1.0, 6.0, ((0, 32),)),
        "pair_tiles": scatter_about(arg_keys[1], (ALL_SLOTS, TILE, TILE), (SLOTS_DEV * TILE * N_VC // (2 * ABT_DEV)) ** -0.5, 0.09375, ((0, 32),)),
        "slot_pairs": draw_slot_pairs(jax.random.fold_in(arg_keys[4], 71), 0),
        "slot_count": draw_slot_count(jax.random.fold_in(arg_keys[4], 71), 0),
    }


def reference(amplitudes, pair_tiles, slot_pairs, slot_count):
    device_total = N_VP * N_VC
    grouped = amplitudes.astype(jnp.float32).reshape(PAIRS, CT_DEV * N_VC, TILE)
    all_tiles = pair_tiles.reshape(device_total, SLOTS_DEV, TILE, TILE)
    all_pairs = slot_pairs.reshape(device_total, SLOTS_DEV, 2)

    def add_device(totals, inputs):
        device_index, tiles_block, slot_table, live_count = inputs
        row_block = device_index // N_VC
        col_block = device_index % N_VC
        cd_index = (col_block * CT_DEV + slot_table[:, 1]).astype(jnp.int32)
        picked = jnp.take(grouped, cd_index, axis=1)
        product = jnp.einsum('pkc,kcn->pkn', picked, tiles_block.astype(jnp.float32), precision=lax.Precision.HIGHEST)
        alive_mask = (jnp.arange(SLOTS_DEV, dtype=jnp.int32) < live_count).astype(jnp.float32)
        select = (slot_table[:, 0][:, None] == jnp.arange(ABT_DEV, dtype=jnp.int32)[None, :]).astype(jnp.float32) * alive_mask[:, None]
        block_sum = jnp.einsum('pkn,ka->pan', product, select, precision=lax.Precision.HIGHEST)
        offset_tile = (row_block * ABT_DEV).astype(jnp.int32)
        current = lax.dynamic_slice_in_dim(totals, offset_tile, ABT_DEV, 1)
        totals = lax.dynamic_update_slice_in_dim(totals, current + block_sum, offset_tile, 1)
        return totals, None

    start_totals = jnp.zeros((PAIRS, ABT_DEV * N_VP, TILE), jnp.float32)
    totals, unused = lax.scan(add_device, start_totals, (jnp.arange(device_total, dtype=jnp.int32), all_tiles, all_pairs, slot_count))
    return totals.reshape(PAIRS, AB).astype(jnp.bfloat16)
```

```python
import functools

import jax
import jax.numpy as jnp
from jax import lax
from jax.experimental import pallas as pl
from jax.experimental.pallas import tpu as pltpu
from jax.sharding import PartitionSpec as P

AB_TILES = 16
SLOW = 4
VMEM = 56 * 1024 * 1024
MESH = pl.DeviceIdType.MESH


def largest_divisor(value, limit):
    return max(d for d in range(1, limit + 1) if value % d == 0)


def gather_kernel(dims, amp_ref, full_ref, pieces, piece_send, piece_recv,
                  up_send, down_send, chain_recv, side_send, side_recv):
    slow, fast, vcs, tiles, chunks = dims
    share = tiles // fast
    size = share // chunks
    group = fast * vcs
    vp = lax.axis_index("vp")
    c = lax.axis_index("vc")
    a, b = lax.div(vp, fast), lax.rem(vp, fast)
    me = b * vcs + c

    def in_plane(step):
        other = lax.rem(me + step, group)
        return lax.div(other, vcs), lax.rem(other, vcs)

    def plane_id(ob, oc):
        return (a * fast + ob, oc)

    barrier = pltpu.get_barrier_semaphore()

    def greet(step, carry):
        ob, oc = in_plane(step)
        pl.semaphore_signal(barrier, inc=1, device_id=plane_id(ob, oc), device_id_type=MESH)
        return carry

    lax.fori_loop(1, group, greet, 0)

    @pl.when(a > 0)
    def _():
        pl.semaphore_signal(barrier, inc=1, device_id=(vp - fast, c), device_id_type=MESH)

    @pl.when(a < slow - 1)
    def _():
        pl.semaphore_signal(barrier, inc=1, device_id=(vp + fast, c), device_id_type=MESH)

    edges = (a > 0).astype(jnp.int32) + (a < slow - 1).astype(jnp.int32)
    pl.semaphore_wait(barrier, group - 1 + edges)

    def piece_copy(k, step):
        ob, oc = in_plane(step)
        return pltpu.make_async_remote_copy(
            src_ref=amp_ref.at[pl.ds(oc * tiles + ob * share + k * size, size)],
            dst_ref=pieces.at[me, pl.ds(k * size, size)],
            send_sem=piece_send, recv_sem=piece_recv.at[k],
            device_id=plane_id(ob, oc), device_id_type=MESH)

    def send_pieces(k, carry):
        def one(step, carry):
            piece_copy(k, step).start()
            return carry
        return lax.fori_loop(1, group, one, carry)

    lax.fori_loop(0, chunks, send_pieces, 0)
    pieces[me] = amp_ref[pl.ds(c * tiles + b * share, share)]

    def block(plane, k):
        return full_ref.at[plane, pl.ds(b * share + k * size, size)]

    def up(plane, k):
        return pltpu.make_async_remote_copy(
            src_ref=block(plane, k), dst_ref=block(plane, k),
            send_sem=up_send.at[plane, k], recv_sem=chain_recv.at[plane, k],
            device_id=(vp + fast, c), device_id_type=MESH)

    def down(plane, k):
        return pltpu.make_async_remote_copy(
            src_ref=block(plane, k), dst_ref=block(plane, k),
            send_sem=down_send.at[plane, k], recv_sem=chain_recv.at[plane, k],
            device_id=(vp - fast, c), device_id_type=MESH)

    def sideways(plane, k):
        def one(step, carry):
            ob = lax.rem(b + step, fast)
            pltpu.make_async_remote_copy(
                src_ref=block(plane, k), dst_ref=block(plane, k),
                send_sem=side_send, recv_sem=side_recv,
                device_id=plane_id(ob, c), device_id_type=MESH).start()
            return carry
        lax.fori_loop(1, fast, one, 0)

    def own_chunk(k, carry):
        arrived = pieces.at[pl.ds(0, group - 1), pl.ds(k * size, size)]
        pltpu.make_async_copy(arrived, arrived, piece_recv.at[k]).wait()
        full_ref[a, pl.ds(b * share + k * size, size)] = jnp.concatenate(
            [pieces[i, pl.ds(k * size, size)] for i in range(group)], axis=1)

        @pl.when(a > 0)
        def _():
            down(a, k).start()

        @pl.when(a < slow - 1)
        def _():
            up(a, k).start()

        sideways(a, k)
        return carry

    lax.fori_loop(0, chunks, own_chunk, 0)

    for far in range(1, slow):
        def passed_chunk(k, carry, far=far):
            @pl.when(a - far >= 0)
            def _():
                up(a - far, k).wait_recv()

                @pl.when(a < slow - 1)
                def _():
                    up(a - far, k).start()

                sideways(a - far, k)

            @pl.when(a + far < slow)
            def _():
                down(a + far, k).wait_recv()

                @pl.when(a > 0)
                def _():
                    down(a + far, k).start()

                sideways(a + far, k)

            return carry

        lax.fori_loop(0, chunks, passed_chunk, 0)

    if fast > 1:
        moved = full_ref.at[:, pl.ds(0, (fast - 1) * share)]
        pltpu.make_async_copy(moved, moved, side_recv).wait()
        pltpu.make_async_copy(moved, moved, side_send).wait()
    sent = pieces.at[pl.ds(0, group - 1)]
    pltpu.make_async_copy(sent, sent, piece_send).wait()

    for far in range(slow):
        def sent_chunk(k, carry, far=far):
            @pl.when((a - far >= 0) & (a < slow - 1))
            def _():
                up(a - far, k).wait_send()

            @pl.when((a + far < slow) & (a > 0))
            def _():
                down(a + far, k).wait_send()

            return carry

        lax.fori_loop(0, chunks, sent_chunk, 0)


def ladder_kernel(batch, parts, pairs_ref, count_ref, full_ref, tiles_hbm, out_ref, tiles, sems):
    slots = tiles.shape[0]
    part = slots // parts
    width = tiles.shape[1]
    rows = full_ref.shape[0] * full_ref.shape[2]
    out_parts, _, out_rows, _ = out_ref.shape

    def fetch(i):
        window = pl.ds(i * part, part)
        return pltpu.make_async_copy(tiles_hbm.at[window], tiles.at[window], sems.at[i])

    for i in range(parts):
        fetch(i).start()
    out_ref[...] = jnp.zeros_like(out_ref)
    count = count_ref[0]
    for i in range(parts):
        fetch(i).wait()

        def step(j, carry, i=i):
            base = i * part + j * batch

            @pl.when(base < count)
            def _():
                products = []
                for n in range(batch):
                    left = full_ref[:, pairs_ref[2 * (base + n) + 1]].reshape(rows, width)
                    products.append(jnp.dot(left, tiles[base + n], preferred_element_type=jnp.float32))
                for n in range(batch):
                    ab = pairs_ref[2 * (base + n)]
                    live = base + n < count
                    term = jnp.where(live, products[n], 0.0).reshape(out_parts, out_rows, width)
                    out_ref[:, ab] += term

            return carry

        lax.fori_loop(0, part // batch, step, 0)


def sum_kernel(parts, part_ref, out_ref, arrived, send_sem, recv_sem):
    c = lax.axis_index("vc")
    vp = lax.axis_index("vp")
    barrier = pltpu.get_barrier_semaphore()
    for step in range(1, parts):
        pl.semaphore_signal(barrier, inc=1, device_id=(vp, lax.rem(c + step, parts)), device_id_type=MESH)
    pl.semaphore_wait(barrier, parts - 1)
    copies = []
    for step in range(1, parts):
        other = lax.rem(c + step, parts)
        copy = pltpu.make_async_remote_copy(
            src_ref=part_ref.at[other], dst_ref=arrived.at[step - 1],
            send_sem=send_sem.at[step - 1], recv_sem=recv_sem.at[step - 1],
            device_id=(vp, other), device_id_type=MESH)
        copy.start()
        copies.append(copy)
    for copy in copies:
        copy.wait_recv()
    width = part_ref.shape[3]
    for i in range(part_ref.shape[1]):
        total = part_ref[c, i]
        for step in range(parts - 1):
            total += arrived[step, i]
        out_ref[:, i * width:(i + 1) * width] = total.astype(out_ref.dtype)
    for copy in copies:
        copy.wait_send()


def per_device(n_vp, n_vc, amplitudes, pair_tiles, slot_pairs, slot_count):
    own_rows, columns = amplitudes.shape
    slots, width, _ = pair_tiles.shape
    slow = SLOW if n_vp % SLOW == 0 else n_vp
    fast = n_vp // slow
    tiles = columns // width // n_vc
    rows = own_rows * n_vp * n_vc
    plane_rows = rows // slow
    share = tiles // fast
    chunks = largest_divisor(share, 5)
    group = fast * n_vc
    in_vmem = pl.BlockSpec(memory_space=pltpu.VMEM)

    amp = amplitudes.reshape(own_rows, columns // width, width).transpose(1, 0, 2)
    full = pl.pallas_call(
        functools.partial(gather_kernel, (slow, fast, n_vc, tiles, chunks)),
        out_shape=jax.ShapeDtypeStruct((slow, tiles, plane_rows, width), amplitudes.dtype),
        in_specs=[in_vmem],
        out_specs=in_vmem,
        scratch_shapes=[
            pltpu.VMEM((group, share, own_rows, width), amplitudes.dtype),
            pltpu.SemaphoreType.DMA,
            pltpu.SemaphoreType.DMA((chunks,)),
            pltpu.SemaphoreType.DMA((slow, chunks)),
            pltpu.SemaphoreType.DMA((slow, chunks)),
            pltpu.SemaphoreType.DMA((slow, chunks)),
            pltpu.SemaphoreType.DMA,
            pltpu.SemaphoreType.DMA,
        ],
        compiler_params=pltpu.CompilerParams(
            collective_id=0, has_side_effects=True, vmem_limit_bytes=VMEM),
        name="gather_amplitudes",
    )(amp)

    out_rows = rows // n_vc
    parts = largest_divisor(slots, 8)
    batch = largest_divisor(slots // parts, max(1, 1024 // rows))
    in_smem = pl.BlockSpec(memory_space=pltpu.SMEM)
    partial = pl.pallas_call(
        functools.partial(ladder_kernel, batch, parts),
        out_shape=jax.ShapeDtypeStruct((n_vc, AB_TILES, out_rows, width), jnp.float32),
        in_specs=[in_smem, in_smem, in_vmem, pl.BlockSpec(memory_space=pl.ANY)],
        out_specs=in_vmem,
        scratch_shapes=[
            pltpu.VMEM(pair_tiles.shape, pair_tiles.dtype),
            pltpu.SemaphoreType.DMA((parts,)),
        ],
        compiler_params=pltpu.CompilerParams(vmem_limit_bytes=VMEM),
        name="ladder",
    )(slot_pairs.reshape(-1), slot_count, full, pair_tiles)

    return pl.pallas_call(
        functools.partial(sum_kernel, n_vc),
        out_shape=jax.ShapeDtypeStruct((out_rows, AB_TILES * width), jnp.bfloat16),
        in_specs=[in_vmem],
        out_specs=in_vmem,
        scratch_shapes=[
            pltpu.VMEM((n_vc - 1, AB_TILES, out_rows, width), jnp.float32),
            pltpu.SemaphoreType.DMA((n_vc - 1,)),
            pltpu.SemaphoreType.DMA((n_vc - 1,)),
        ],
        compiler_params=pltpu.CompilerParams(
            collective_id=1, has_side_effects=True, vmem_limit_bytes=VMEM),
        name="sum_partials",
    )(partial)


def solution(mesh):
    in_specs = (
        P(("vp", "vc"), None),
        P(("vp", "vc"), None, None),
        P(("vp", "vc"), None),
        P(("vp", "vc")),
    )
    return jax.shard_map(
        functools.partial(per_device, mesh.shape["vp"], mesh.shape["vc"]),
        mesh=mesh, in_specs=in_specs, out_specs=P("vc", "vp"), check_vma=False)
```

```python
import functools
import math

import jax
import jax.numpy as jnp
from jax import lax
from jax.experimental import pallas as pl
from jax.experimental.pallas import tpu as pltpu
from jax.sharding import PartitionSpec as P

AB_TILES = 16
SLOW = 4
VMEM = 56 * 1024 * 1024
MESH = pl.DeviceIdType.MESH


def largest_divisor(value, limit):
    return max(d for d in range(1, limit + 1) if value % d == 0)


def gather_kernel(dims, amp_ref, full_ref, pieces, piece_send, piece_recv,
                  up_send, down_send, chain_recv, side_send, side_recv):
    slow, fast, vcs, tiles, shared, size = dims
    share = (tiles - shared) // fast
    held = share + shared
    own_chunks, chunks = share // size, held // size
    group = fast * vcs
    vp = lax.axis_index("vp")
    c = lax.axis_index("vc")
    a, b = lax.div(vp, fast), lax.rem(vp, fast)
    me = b * vcs + c

    def in_plane(step):
        other = lax.rem(me + step, group)
        return lax.div(other, vcs), lax.rem(other, vcs)

    def plane_id(ob, oc):
        return (a * fast + ob, oc)

    def tile_at(ob, k):
        return jnp.where(k < own_chunks, ob * share + k * size, fast * share + (k - own_chunks) * size)

    barrier = pltpu.get_barrier_semaphore()

    def greet(step, carry):
        ob, oc = in_plane(step)
        pl.semaphore_signal(barrier, inc=1, device_id=plane_id(ob, oc), device_id_type=MESH)
        return carry

    lax.fori_loop(1, group, greet, 0)

    @pl.when(a > 0)
    def _():
        pl.semaphore_signal(barrier, inc=1, device_id=(vp - fast, c), device_id_type=MESH)

    @pl.when(a < slow - 1)
    def _():
        pl.semaphore_signal(barrier, inc=1, device_id=(vp + fast, c), device_id_type=MESH)

    edges = (a > 0).astype(jnp.int32) + (a < slow - 1).astype(jnp.int32)
    pl.semaphore_wait(barrier, group - 1 + edges)

    def send_pieces(k, carry):
        def one(step, carry):
            ob, oc = in_plane(step)
            pltpu.make_async_remote_copy(
                src_ref=amp_ref.at[pl.ds(oc * tiles + tile_at(ob, k), size)],
                dst_ref=pieces.at[me, pl.ds(k * size, size)],
                send_sem=piece_send, recv_sem=piece_recv.at[k],
                device_id=plane_id(ob, oc), device_id_type=MESH).start()
            return carry
        return lax.fori_loop(1, group, one, carry)

    lax.fori_loop(0, chunks, send_pieces, 0)
    pieces[me, :share] = amp_ref[pl.ds(c * tiles + b * share, share)]
    if shared:
        pieces[me, share:] = amp_ref[pl.ds(c * tiles + fast * share, shared)]

    def block(plane, k):
        return full_ref.at[plane, pl.ds(tile_at(b, k), size)]

    def up(plane, k):
        return pltpu.make_async_remote_copy(
            src_ref=block(plane, k), dst_ref=block(plane, k),
            send_sem=up_send.at[plane, k], recv_sem=chain_recv.at[plane, k],
            device_id=(vp + fast, c), device_id_type=MESH)

    def down(plane, k):
        return pltpu.make_async_remote_copy(
            src_ref=block(plane, k), dst_ref=block(plane, k),
            send_sem=down_send.at[plane, k], recv_sem=chain_recv.at[plane, k],
            device_id=(vp - fast, c), device_id_type=MESH)

    def sideways(plane, k):
        def one(step, carry):
            ob = lax.rem(b + step, fast)
            pltpu.make_async_remote_copy(
                src_ref=block(plane, k), dst_ref=block(plane, k),
                send_sem=side_send, recv_sem=side_recv,
                device_id=plane_id(ob, c), device_id_type=MESH).start()
            return carry
        lax.fori_loop(1, fast, one, 0)

    def own_chunk(k, side):
        arrived = pieces.at[pl.ds(0, group - 1), pl.ds(k * size, size)]
        pltpu.make_async_copy(arrived, arrived, piece_recv.at[k]).wait()
        full_ref[a, pl.ds(tile_at(b, k), size)] = jnp.concatenate(
            [pieces[i, pl.ds(k * size, size)] for i in range(group)], axis=1)

        @pl.when(a > 0)
        def _():
            down(a, k).start()

        @pl.when(a < slow - 1)
        def _():
            up(a, k).start()

        if side:
            sideways(a, k)

    def passed_chunk(far, k, side):
        @pl.when(a - far >= 0)
        def _():
            up(a - far, k).wait_recv()

            @pl.when(a < slow - 1)
            def _():
                up(a - far, k).start()

            if side:
                sideways(a - far, k)

        @pl.when(a + far < slow)
        def _():
            down(a + far, k).wait_recv()

            @pl.when(a > 0)
            def _():
                down(a + far, k).start()

            if side:
                sideways(a + far, k)

    for first, last, side in ((0, own_chunks, True), (own_chunks, chunks, False)):
        if first == last:
            continue

        def own(k, carry, side=side):
            own_chunk(k, side)
            return carry

        lax.fori_loop(first, last, own, 0)
        for far in range(1, slow):
            def passed(k, carry, far=far, side=side):
                passed_chunk(far, k, side)
                return carry

            lax.fori_loop(first, last, passed, 0)

    if fast > 1:
        moved = full_ref.at[:, pl.ds(0, (fast - 1) * share)]
        pltpu.make_async_copy(moved, moved, side_recv).wait()
        pltpu.make_async_copy(moved, moved, side_send).wait()
    sent = pieces.at[pl.ds(0, group - 1)]
    pltpu.make_async_copy(sent, sent, piece_send).wait()

    for far in range(slow):
        def sent_chunk(k, carry, far=far):
            @pl.when((a - far >= 0) & (a < slow - 1))
            def _():
                up(a - far, k).wait_send()

            @pl.when((a + far < slow) & (a > 0))
            def _():
                down(a + far, k).wait_send()

            return carry

        lax.fori_loop(0, chunks, sent_chunk, 0)


def ladder_kernel(batch, parts, pairs_ref, count_ref, full_ref, tiles_hbm, out_ref, tiles, sems):
    slots = tiles.shape[0]
    part = slots // parts
    width = tiles.shape[1]
    rows = full_ref.shape[0] * full_ref.shape[2]
    out_parts, _, out_rows, _ = out_ref.shape

    def fetch(i):
        window = pl.ds(i * part, part)
        return pltpu.make_async_copy(tiles_hbm.at[window], tiles.at[window], sems.at[i])

    for i in range(parts):
        fetch(i).start()
    out_ref[...] = jnp.zeros_like(out_ref)
    count = count_ref[0]
    for i in range(parts):
        fetch(i).wait()

        def step(j, carry, i=i):
            base = i * part + j * batch

            @pl.when(base < count)
            def _():
                products = []
                for n in range(batch):
                    left = full_ref[:, pairs_ref[1, base + n]].reshape(rows, width)
                    products.append(jnp.dot(left, tiles[base + n], preferred_element_type=jnp.float32))
                for n in range(batch):
                    ab = pairs_ref[0, base + n]
                    live = base + n < count
                    term = jnp.where(live, products[n], 0.0).reshape(out_parts, out_rows, width)
                    out_ref[:, ab] += term

            return carry

        lax.fori_loop(0, part // batch, step, 0)


def sum_kernel(pair, pieces, part_ref, out_ref, near, sums, far, near_send, near_recv, far_send, far_recv):
    parts, ab_tiles, _, width = part_ref.shape
    outer = parts // pair
    size = ab_tiles // pieces
    c = lax.axis_index("vc")
    vp = lax.axis_index("vp")
    y, core = lax.div(c, pair), lax.rem(c, pair)
    barrier = pltpu.get_barrier_semaphore()

    def other_y(step):
        return lax.rem(y + step, outer)

    peers = [other_y(step) * pair + core for step in range(1, outer)]
    if pair == 2:
        peers.append(y * pair + 1 - core)
    for peer in peers:
        pl.semaphore_signal(barrier, inc=1, device_id=(vp, peer), device_id_type=MESH)
    pl.semaphore_wait(barrier, len(peers))

    steps = list(range(1, outer)) + [0]
    waits = []
    nears = {}
    if pair == 2:
        for step in steps:
            i = other_y(step)
            for h in range(pieces):
                copy = pltpu.make_async_remote_copy(
                    src_ref=part_ref.at[i * pair + 1 - core, pl.ds(h * size, size)],
                    dst_ref=near.at[i, pl.ds(h * size, size)],
                    send_sem=near_send.at[step, h], recv_sem=near_recv.at[step, h],
                    device_id=(vp, y * pair + 1 - core), device_id_type=MESH)
                copy.start()
                nears[step, h] = copy
                waits.append(copy)

    def chip_sum(step, h):
        i = other_y(step)
        window = pl.ds(h * size, size)
        value = part_ref[i * pair + core, window]
        if pair == 2:
            nears[step, h].wait_recv()
            value = value + near[i, window]
        return i, window, value

    fars = {}
    for h in range(pieces):
        for step in steps[:-1]:
            i, window, value = chip_sum(step, h)
            sums[i, window] = value
            copy = pltpu.make_async_remote_copy(
                src_ref=sums.at[i, window], dst_ref=far.at[step - 1, window],
                send_sem=far_send.at[step - 1, h], recv_sem=far_recv.at[step - 1, h],
                device_id=(vp, i * pair + core), device_id_type=MESH)
            copy.start()
            fars[step, h] = copy
            waits.append(copy)
    for h in range(pieces):
        _, window, total = chip_sum(0, h)
        for step in steps[:-1]:
            fars[step, h].wait_recv()
            total = total + far[step - 1, window]
        for n in range(size):
            at = (h * size + n) * width
            out_ref[:, at:at + width] = total[n].astype(out_ref.dtype)
    for copy in waits:
        copy.wait_send()


def per_device(n_vp, n_vc, amplitudes, pair_tiles, slot_pairs, slot_count):
    own_rows, columns = amplitudes.shape
    slots, width, _ = pair_tiles.shape
    slow = SLOW if n_vp % SLOW == 0 else n_vp
    fast = n_vp // slow
    tiles = columns // width // n_vc
    rows = own_rows * n_vp * n_vc
    plane_rows = rows // slow
    shared = tiles // 5
    shared += (tiles - shared) % fast
    share = (tiles - shared) // fast
    size = largest_divisor(math.gcd(share, shared), 20)
    chunks = (share + shared) // size
    group = fast * n_vc
    in_vmem = pl.BlockSpec(memory_space=pltpu.VMEM)

    amp = amplitudes.reshape(own_rows, columns // width, width).transpose(1, 0, 2)
    full = pl.pallas_call(
        functools.partial(gather_kernel, (slow, fast, n_vc, tiles, shared, size)),
        out_shape=jax.ShapeDtypeStruct((slow, tiles, plane_rows, width), amplitudes.dtype),
        in_specs=[in_vmem],
        out_specs=in_vmem,
        scratch_shapes=[
            pltpu.VMEM((group, share + shared, own_rows, width), amplitudes.dtype),
            pltpu.SemaphoreType.DMA,
            pltpu.SemaphoreType.DMA((chunks,)),
            pltpu.SemaphoreType.DMA((slow, chunks)),
            pltpu.SemaphoreType.DMA((slow, chunks)),
            pltpu.SemaphoreType.DMA((slow, chunks)),
            pltpu.SemaphoreType.DMA,
            pltpu.SemaphoreType.DMA,
        ],
        compiler_params=pltpu.CompilerParams(
            collective_id=0, has_side_effects=True, vmem_limit_bytes=VMEM),
        name="gather_amplitudes",
    )(amp)

    out_rows = rows // n_vc
    parts = largest_divisor(slots, 8)
    batch = largest_divisor(slots // parts, max(1, 1024 // rows))
    in_smem = pl.BlockSpec(memory_space=pltpu.SMEM)
    partial = pl.pallas_call(
        functools.partial(ladder_kernel, batch, parts),
        out_shape=jax.ShapeDtypeStruct((n_vc, AB_TILES, out_rows, width), jnp.float32),
        in_specs=[in_smem, in_smem, in_vmem, pl.BlockSpec(memory_space=pl.ANY)],
        out_specs=in_vmem,
        scratch_shapes=[
            pltpu.VMEM(pair_tiles.shape, pair_tiles.dtype),
            pltpu.SemaphoreType.DMA((parts,)),
        ],
        compiler_params=pltpu.CompilerParams(vmem_limit_bytes=VMEM),
        name="ladder",
    )(slot_pairs.T, slot_count, full, pair_tiles)

    pair = 2 if n_vc % 2 == 0 else 1
    outer = n_vc // pair
    pieces = largest_divisor(AB_TILES, 4)
    block = (AB_TILES, out_rows, width)
    return pl.pallas_call(
        functools.partial(sum_kernel, pair, pieces),
        out_shape=jax.ShapeDtypeStruct((out_rows, AB_TILES * width), jnp.bfloat16),
        in_specs=[in_vmem],
        out_specs=in_vmem,
        scratch_shapes=[
            pltpu.VMEM((outer,) + block, jnp.float32),
            pltpu.VMEM((outer,) + block, jnp.float32),
            pltpu.VMEM((max(outer - 1, 1),) + block, jnp.float32),
            pltpu.SemaphoreType.DMA((outer, pieces)),
            pltpu.SemaphoreType.DMA((outer, pieces)),
            pltpu.SemaphoreType.DMA((outer, pieces)),
            pltpu.SemaphoreType.DMA((outer, pieces)),
        ],
        compiler_params=pltpu.CompilerParams(
            collective_id=1, has_side_effects=True, vmem_limit_bytes=VMEM),
        name="sum_partials",
    )(partial)


def solution(mesh):
    in_specs = (
        P(("vp", "vc"), None),
        P(("vp", "vc"), None, None),
        P(("vp", "vc"), None),
        P(("vp", "vc")),
    )
    return jax.shard_map(
        functools.partial(per_device, mesh.shape["vp"], mesh.shape["vc"]),
        mesh=mesh, in_specs=in_specs, out_specs=P("vc", "vp"), check_vma=False)
```

```python
import functools
import math

import jax
import jax.numpy as jnp
from jax import lax
from jax.experimental import pallas as pl
from jax.experimental.pallas import tpu as pltpu
from jax.sharding import PartitionSpec as P

AB_TILES = 16
SLOW = 4
VMEM = 60 * 1024 * 1024
MESH = pl.DeviceIdType.MESH


def largest_divisor(value, limit):
    return max(d for d in range(1, limit + 1) if value % d == 0)


def gather(dims, amp_ref, full_ref, pieces, piece_send, piece_recv,
           up_send, down_send, chain_recv, side_send, side_recv, meanwhile):
    slow, fast, vcs, tiles, shared, size = dims
    share = (tiles - shared) // fast
    held = share + shared
    own_chunks, chunks = share // size, held // size
    group = fast * vcs
    vp = lax.axis_index("vp")
    c = lax.axis_index("vc")
    a, b = lax.div(vp, fast), lax.rem(vp, fast)
    me = b * vcs + c

    def in_plane(step):
        other = lax.rem(me + step, group)
        return lax.div(other, vcs), lax.rem(other, vcs)

    def plane_id(ob, oc):
        return (a * fast + ob, oc)

    def tile_at(ob, k):
        return jnp.where(k < own_chunks, ob * share + k * size, fast * share + (k - own_chunks) * size)

    barrier = pltpu.get_barrier_semaphore()

    def greet(step, carry):
        ob, oc = in_plane(step)
        pl.semaphore_signal(barrier, inc=1, device_id=plane_id(ob, oc), device_id_type=MESH)
        return carry

    lax.fori_loop(1, group, greet, 0)

    @pl.when(a > 0)
    def _():
        pl.semaphore_signal(barrier, inc=1, device_id=(vp - fast, c), device_id_type=MESH)

    @pl.when(a < slow - 1)
    def _():
        pl.semaphore_signal(barrier, inc=1, device_id=(vp + fast, c), device_id_type=MESH)

    edges = (a > 0).astype(jnp.int32) + (a < slow - 1).astype(jnp.int32)
    pl.semaphore_wait(barrier, group - 1 + edges)

    def send_pieces(k, carry):
        def one(step, carry):
            ob, oc = in_plane(step)
            pltpu.make_async_remote_copy(
                src_ref=amp_ref.at[pl.ds(oc * tiles + tile_at(ob, k), size)],
                dst_ref=pieces.at[me, pl.ds(k * size, size)],
                send_sem=piece_send, recv_sem=piece_recv.at[k],
                device_id=plane_id(ob, oc), device_id_type=MESH).start()
            return carry
        return lax.fori_loop(1, group, one, carry)

    ahead = min(2, chunks)
    lax.fori_loop(0, ahead, send_pieces, 0)
    pieces[me, :share] = amp_ref[pl.ds(c * tiles + b * share, share)]
    if shared:
        pieces[me, share:] = amp_ref[pl.ds(c * tiles + fast * share, shared)]

    meanwhile()

    def block(plane, k):
        return full_ref.at[plane, pl.ds(tile_at(b, k), size)]

    def up(plane, k):
        return pltpu.make_async_remote_copy(
            src_ref=block(plane, k), dst_ref=block(plane, k),
            send_sem=up_send.at[plane, k], recv_sem=chain_recv.at[plane, k],
            device_id=(vp + fast, c), device_id_type=MESH)

    def down(plane, k):
        return pltpu.make_async_remote_copy(
            src_ref=block(plane, k), dst_ref=block(plane, k),
            send_sem=down_send.at[plane, k], recv_sem=chain_recv.at[plane, k],
            device_id=(vp - fast, c), device_id_type=MESH)

    def sideways(plane, k):
        def one(step, carry):
            ob = lax.rem(b + step, fast)
            pltpu.make_async_remote_copy(
                src_ref=block(plane, k), dst_ref=block(plane, k),
                send_sem=side_send, recv_sem=side_recv,
                device_id=plane_id(ob, c), device_id_type=MESH).start()
            return carry
        lax.fori_loop(1, fast, one, 0)

    def own_chunk(k, side):
        arrived = pieces.at[pl.ds(0, group - 1), pl.ds(k * size, size)]
        pltpu.make_async_copy(arrived, arrived, piece_recv.at[k]).wait()
        full_ref[a, pl.ds(tile_at(b, k), size)] = jnp.concatenate(
            [pieces[i, pl.ds(k * size, size)] for i in range(group)], axis=1)

        @pl.when(a > 0)
        def _():
            down(a, k).start()

        @pl.when(a < slow - 1)
        def _():
            up(a, k).start()

        if side:
            sideways(a, k)

        @pl.when(k + ahead < chunks)
        def _():
            send_pieces(k + ahead, 0)

    def passed_chunk(far, k, side):
        @pl.when(a - far >= 0)
        def _():
            up(a - far, k).wait_recv()

            @pl.when(a < slow - 1)
            def _():
                up(a - far, k).start()

            if side:
                sideways(a - far, k)

        @pl.when(a + far < slow)
        def _():
            down(a + far, k).wait_recv()

            @pl.when(a > 0)
            def _():
                down(a + far, k).start()

            if side:
                sideways(a + far, k)

    for first, last, side in ((0, own_chunks, True), (own_chunks, chunks, False)):
        if first == last:
            continue

        def own(k, carry, side=side):
            own_chunk(k, side)
            return carry

        lax.fori_loop(first, last, own, 0)
        for far in range(1, slow):
            def passed(k, carry, far=far, side=side):
                passed_chunk(far, k, side)
                return carry

            lax.fori_loop(first, last, passed, 0)

    if fast > 1:
        moved = full_ref.at[:, pl.ds(0, (fast - 1) * share)]
        pltpu.make_async_copy(moved, moved, side_recv).wait()


def gather_sends(dims, full_ref, pieces, piece_send, up_send, down_send, side_send):
    slow, fast, vcs, tiles, shared, size = dims
    share = (tiles - shared) // fast
    chunks = (share + shared) // size
    group = fast * vcs
    a = lax.div(lax.axis_index("vp"), fast)
    one = full_ref.at[0, pl.ds(0, size)]
    if fast > 1:
        moved = full_ref.at[:, pl.ds(0, (fast - 1) * share)]
        pltpu.make_async_copy(moved, moved, side_send).wait()
    sent = pieces.at[pl.ds(0, group - 1)]
    pltpu.make_async_copy(sent, sent, piece_send).wait()

    for far in range(slow):
        def sent_chunk(k, carry, far=far):
            @pl.when((a - far >= 0) & (a < slow - 1))
            def _():
                pltpu.make_async_copy(one, one, up_send.at[a - far, k]).wait()

            @pl.when((a + far < slow) & (a > 0))
            def _():
                pltpu.make_async_copy(one, one, down_send.at[a + far, k]).wait()

            return carry

        lax.fori_loop(0, chunks, sent_chunk, 0)


def sum_partials(pair, pieces, part_ref, out_ref, near, sums, far, near_send, near_recv, far_send, far_recv):
    parts, ab_tiles, _, width = part_ref.shape
    outer = parts // pair
    size = ab_tiles // pieces
    c = lax.axis_index("vc")
    vp = lax.axis_index("vp")
    y, core = lax.div(c, pair), lax.rem(c, pair)

    def other_y(step):
        return lax.rem(y + step, outer)

    steps = list(range(1, outer)) + [0]
    waits = []
    nears = {}
    if pair == 2:
        for step in steps:
            i = other_y(step)
            for h in range(pieces):
                copy = pltpu.make_async_remote_copy(
                    src_ref=part_ref.at[i * pair + 1 - core, pl.ds(h * size, size)],
                    dst_ref=near.at[i, pl.ds(h * size, size)],
                    send_sem=near_send.at[step, h], recv_sem=near_recv.at[step, h],
                    device_id=(vp, y * pair + 1 - core), device_id_type=MESH)
                copy.start()
                nears[step, h] = copy
                waits.append(copy)

    def chip_sum(step, h):
        i = other_y(step)
        window = pl.ds(h * size, size)
        value = part_ref[i * pair + core, window]
        if pair == 2:
            nears[step, h].wait_recv()
            value = value + near[i, window]
        return i, window, value

    fars = {}
    for h in range(pieces):
        for step in steps[:-1]:
            i, window, value = chip_sum(step, h)
            sums[i, window] = value
            copy = pltpu.make_async_remote_copy(
                src_ref=sums.at[i, window], dst_ref=far.at[step - 1, window],
                send_sem=far_send.at[step - 1, h], recv_sem=far_recv.at[step - 1, h],
                device_id=(vp, i * pair + core), device_id_type=MESH)
            copy.start()
            fars[step, h] = copy
            waits.append(copy)
    for h in range(pieces):
        _, window, total = chip_sum(0, h)
        for step in steps[:-1]:
            fars[step, h].wait_recv()
            total = total + far[step - 1, window]
        for n in range(size):
            at = (h * size + n) * width
            out_ref[:, at:at + width] = total[n].astype(out_ref.dtype)
    for copy in waits:
        copy.wait_send()


def sort_slots(count, pairs_ref, table):
    slots = pairs_ref.shape[1]
    ab_row = pairs_ref[0:1, :]
    rows = lax.broadcasted_iota(jnp.int32, (slots, slots), 0)
    lanes = lax.broadcasted_iota(jnp.int32, (slots, slots), 1)

    def as_column(row):
        return jnp.sum(jnp.where(rows == lanes, row, 0), axis=1, keepdims=True)

    slot_row = lax.broadcasted_iota(jnp.int32, (1, slots), 1)
    key_row = jnp.where(slot_row < count, ab_row, AB_TILES) * slots + slot_row
    key_col = as_column(key_row)
    rank_col = jnp.sum((key_row < key_col).astype(jnp.int32), axis=1, keepdims=True)
    chosen = rank_col == lanes

    def in_order(column):
        return jnp.sum(jnp.where(chosen, column, 0), axis=0, keepdims=True)

    table[...] = jnp.zeros_like(table)
    table[0:1, :] = in_order(rows[:, 0:1])
    table[1:2, :] = in_order(as_column(pairs_ref[1:2, :]))
    key_sorted = in_order(key_col)
    same = jnp.any((rank_col + 1 == lanes) & (lax.div(key_col, slots) == lax.div(key_sorted, slots)),
                   axis=0, keepdims=True)
    table[2:3, :] = same.astype(jnp.int32)
    table[3:4, :] = jnp.sum((key_col < (lanes + 1) * slots).astype(jnp.int32), axis=0, keepdims=True)


def multiply(planes, first_row, row_count, batch, smem, full_ref, tiles, running):
    slots, width = tiles.shape[0], tiles.shape[1]
    rows = planes.size * row_count

    def step(j, total):
        base = j * batch
        products = []
        for n in range(batch):
            left = full_ref[planes, smem[1, base + n], pl.ds(first_row, row_count)]
            products.append(jnp.dot(left.reshape(rows, width), tiles[smem[0, base + n]],
                                    preferred_element_type=jnp.float32))
        for n in range(batch):
            total = total * smem[2, base + n].astype(jnp.float32) + products[n]
            running[base + n] = total
        return total

    lax.fori_loop(0, slots // batch, step, jnp.zeros((rows, width), jnp.float32))


def last_totals(ab, smem, running):
    end = smem[3, ab]
    start = smem[3, ab - 1] if ab else 0
    some = jnp.minimum(end - start, 1).astype(jnp.float32)
    return running[jnp.maximum(end - 1, 0)] * some


def ladder_kernel(dims, batch, pieces_n, pair, count_ref, pairs_ref, amp_ref, tiles_hbm, out_ref,
                  full, pieces, tiles, running, partial, near, sums, far, table, smem,
                  piece_send, piece_recv, up_send, down_send, chain_recv, side_send, side_recv,
                  tile_sem, table_sem, near_send, near_recv, far_send, far_recv):
    slow, plane_rows = full.shape[0], full.shape[2]
    out_rows = partial.shape[2]
    width = tiles.shape[2]

    def meanwhile():
        pltpu.make_async_copy(tiles_hbm, tiles, tile_sem).start()
        sort_slots(count_ref[0], pairs_ref, table)
        pltpu.make_async_copy(table, smem, table_sem).start()

    gather(dims, amp_ref, full, pieces, piece_send, piece_recv,
           up_send, down_send, chain_recv, side_send, side_recv, meanwhile)
    pltpu.make_async_copy(tiles_hbm, tiles, tile_sem).wait()
    pltpu.make_async_copy(table, smem, table_sem).wait()

    at_once = running.shape[1]
    row_count = min(at_once, plane_rows)
    planes = at_once // row_count
    for plane in range(0, slow, planes):
        for row in range(0, plane_rows, row_count):
            multiply(pl.ds(plane, planes), row, row_count, batch, smem, full, tiles, running)
            target = (plane * plane_rows + row) // out_rows
            for ab in range(AB_TILES):
                partial[target:target + at_once // out_rows, ab] = last_totals(
                    ab, smem, running).reshape(at_once // out_rows, out_rows, width)

    sum_partials(pair, pieces_n, partial, out_ref, near, sums, far, near_send, near_recv, far_send, far_recv)
    gather_sends(dims, full, pieces, piece_send, up_send, down_send, side_send)


def per_device(n_vp, n_vc, amplitudes, pair_tiles, slot_pairs, slot_count):
    own_rows, columns = amplitudes.shape
    slots, width, _ = pair_tiles.shape
    slow = SLOW if n_vp % SLOW == 0 else n_vp
    fast = n_vp // slow
    tiles = columns // width // n_vc
    rows = own_rows * n_vp * n_vc
    plane_rows = rows // slow
    shared = tiles // 5
    shared += (tiles - shared) % fast
    share = (tiles - shared) // fast
    size = largest_divisor(math.gcd(share, shared), 20)
    chunks = (share + shared) // size
    group = fast * n_vc
    in_vmem = pl.BlockSpec(memory_space=pltpu.VMEM)

    amp = amplitudes.reshape(own_rows, columns // width, width).transpose(1, 0, 2)
    out_rows = rows // n_vc
    at_once = min(rows, 64)
    slots_batch = largest_divisor(slots, 16)
    pair = 2 if n_vc % 2 == 0 else 1
    outer = n_vc // pair
    parts = largest_divisor(AB_TILES, 4)
    block = (AB_TILES, out_rows, width)
    dma = pltpu.SemaphoreType.DMA
    in_smem = pl.BlockSpec(memory_space=pltpu.SMEM)
    return pl.pallas_call(
        functools.partial(
            ladder_kernel, (slow, fast, n_vc, tiles, shared, size), slots_batch, parts, pair),
        out_shape=jax.ShapeDtypeStruct((out_rows, AB_TILES * width), jnp.bfloat16),
        in_specs=[in_smem, in_vmem, in_vmem, pl.BlockSpec(memory_space=pl.ANY)],
        out_specs=in_vmem,
        scratch_shapes=[
            pltpu.VMEM((slow, tiles, plane_rows, width), amplitudes.dtype),
            pltpu.VMEM((group, share + shared, own_rows, width), amplitudes.dtype),
            pltpu.VMEM(pair_tiles.shape, pair_tiles.dtype),
            pltpu.VMEM((slots, at_once, width), jnp.float32),
            pltpu.VMEM((n_vc,) + block, jnp.float32),
            pltpu.VMEM((outer,) + block, jnp.float32),
            pltpu.VMEM((outer,) + block, jnp.float32),
            pltpu.VMEM((max(outer - 1, 1),) + block, jnp.float32),
            pltpu.VMEM((8, slots), jnp.int32),
            pltpu.SMEM((8, slots), jnp.int32),
            dma, dma((chunks,)),
            dma((slow, chunks)), dma((slow, chunks)), dma((slow, chunks)),
            dma, dma, dma, dma,
            dma((outer, parts)), dma((outer, parts)), dma((outer, parts)), dma((outer, parts)),
        ],
        compiler_params=pltpu.CompilerParams(
            collective_id=0, has_side_effects=True, vmem_limit_bytes=VMEM),
        name="ladder",
    )(slot_count, slot_pairs.T, amp, pair_tiles)


def solution(mesh):
    in_specs = (
        P(("vp", "vc"), None),
        P(("vp", "vc"), None, None),
        P(("vp", "vc"), None),
        P(("vp", "vc")),
    )
    return jax.shard_map(
        functools.partial(per_device, mesh.shape["vp"], mesh.shape["vc"]),
        mesh=mesh, in_specs=in_specs, out_specs=P("vc", "vp"), check_vma=False)
```

```python
import functools
import math

import jax
import jax.numpy as jnp
from jax import lax
from jax.experimental import pallas as pl
from jax.experimental.pallas import tpu as pltpu
from jax.sharding import PartitionSpec as P

AB_TILES = 16
SLOW = 4
PAIR = 2
VMEM = 60 * 1024 * 1024
MESH = pl.DeviceIdType.MESH


def largest_divisor(value, limit):
    return max(d for d in range(1, limit + 1) if value % d == 0)


def gather(dims, amp_ref, full_ref, late_ref, pieces, piece_send, piece_recv,
           up_send, down_send, chain_recv, side_send, side_recv, meanwhile):
    slow, fast, vcs, tiles, shared, size = dims
    share = (tiles - shared) // fast
    held = share + shared
    own_chunks, chunks = share // size, held // size
    group = fast * vcs
    vp = lax.axis_index("vp")
    c = lax.axis_index("vc")
    a, b = lax.div(vp, fast), lax.rem(vp, fast)
    me = b * vcs + c

    def in_plane(step):
        other = lax.rem(me + step, group)
        return lax.div(other, vcs), lax.rem(other, vcs)

    def plane_id(ob, oc):
        return (a * fast + ob, oc)

    def tile_at(ob, k):
        return jnp.where(k < own_chunks, ob * share + k * size, fast * share + (k - own_chunks) * size)

    barrier = pltpu.get_barrier_semaphore()

    def greet(step, carry):
        ob, oc = in_plane(step)
        pl.semaphore_signal(barrier, inc=1, device_id=plane_id(ob, oc), device_id_type=MESH)
        return carry

    lax.fori_loop(1, group, greet, 0)

    @pl.when(a > 0)
    def _():
        pl.semaphore_signal(barrier, inc=1, device_id=(vp - fast, c), device_id_type=MESH)

    @pl.when(a < slow - 1)
    def _():
        pl.semaphore_signal(barrier, inc=1, device_id=(vp + fast, c), device_id_type=MESH)

    edges = (a > 0).astype(jnp.int32) + (a < slow - 1).astype(jnp.int32)
    pl.semaphore_wait(barrier, group - 1 + edges)

    def send_pieces(k, carry):
        def one(step, carry):
            ob, oc = in_plane(step)
            pltpu.make_async_remote_copy(
                src_ref=amp_ref.at[pl.ds(oc * tiles + tile_at(ob, k), size)],
                dst_ref=pieces.at[me, pl.ds(k * size, size)],
                send_sem=piece_send, recv_sem=piece_recv.at[k],
                device_id=plane_id(ob, oc), device_id_type=MESH).start()
            return carry
        return lax.fori_loop(1, group, one, carry)

    ahead = min(2, chunks)
    lax.fori_loop(0, ahead, send_pieces, 0)
    pieces[me, :share] = amp_ref[pl.ds(c * tiles + b * share, share)]
    if shared:
        pieces[me, share:] = amp_ref[pl.ds(c * tiles + fast * share, shared)]

    def start_copy(plane, k, from_a, to_a, send_sem, recv_sem, device):
        window = pl.ds(tile_at(b, k), size)
        from_late, to_late = plane == last_plane(from_a, slow), plane == last_plane(to_a, slow)

        def place(is_late, at_a):
            return late_ref.at[window] if is_late else full_ref.at[plane - first_plane(at_a, slow), window]

        for source in (False, True):
            for target in (False, True):
                @pl.when((from_late == source) & (to_late == target))
                def _(source=source, target=target):
                    pltpu.make_async_remote_copy(
                        src_ref=place(source, from_a), dst_ref=place(target, to_a),
                        send_sem=send_sem, recv_sem=recv_sem,
                        device_id=device, device_id_type=MESH).start()

    def up(plane, k):
        start_copy(plane, k, a, a + 1, up_send.at[plane, k], chain_recv.at[plane, k], (vp + fast, c))

    def down(plane, k):
        start_copy(plane, k, a, a - 1, down_send.at[plane, k], chain_recv.at[plane, k], (vp - fast, c))

    def arrived(plane, k):
        one = late_ref.at[pl.ds(0, size)]
        pltpu.make_async_copy(one, one, chain_recv.at[plane, k]).wait()

    def sideways(plane, k):
        window = pl.ds(tile_at(b, k), size)
        is_late = plane == last_plane(a, slow)

        def one(step, carry):
            ob = lax.rem(b + step, fast)

            @pl.when(is_late)
            def _():
                pltpu.make_async_remote_copy(
                    src_ref=late_ref.at[window], dst_ref=late_ref.at[window],
                    send_sem=side_send.at[1], recv_sem=side_recv.at[1],
                    device_id=plane_id(ob, c), device_id_type=MESH).start()

            @pl.when(jnp.logical_not(is_late))
            def _():
                place = full_ref.at[plane - first_plane(a, slow), window]
                pltpu.make_async_remote_copy(
                    src_ref=place, dst_ref=place,
                    send_sem=side_send.at[0], recv_sem=side_recv.at[0],
                    device_id=plane_id(ob, c), device_id_type=MESH).start()

            return carry

        lax.fori_loop(1, fast, one, 0)

    def own_chunk(k, side):
        landed = pieces.at[pl.ds(0, group - 1), pl.ds(k * size, size)]
        pltpu.make_async_copy(landed, landed, piece_recv.at[k]).wait()
        full_ref[a - first_plane(a, slow), pl.ds(tile_at(b, k), size)] = jnp.concatenate(
            [pieces[i, pl.ds(k * size, size)] for i in range(group)], axis=1)

        @pl.when(a > 0)
        def _():
            down(a, k)

        @pl.when(a < slow - 1)
        def _():
            up(a, k)

        if side:
            sideways(a, k)

        @pl.when(k + ahead < chunks)
        def _():
            send_pieces(k + ahead, 0)

    def passed_chunk(far, k, side):
        @pl.when(a - far >= 0)
        def _():
            arrived(a - far, k)

            @pl.when(a < slow - 1)
            def _():
                up(a - far, k)

            if side:
                sideways(a - far, k)

        @pl.when(a + far < slow)
        def _():
            arrived(a + far, k)

            @pl.when(a > 0)
            def _():
                down(a + far, k)

            if side:
                sideways(a + far, k)

    for first, last, side in ((0, own_chunks, True), (own_chunks, chunks, False)):
        if first == last:
            continue

        def own(k, carry, side=side):
            own_chunk(k, side)
            return carry

        lax.fori_loop(first, last, own, 0)
        if first == 0:
            meanwhile()
        for far in range(1, slow if side else slow - 1):
            def passed(k, carry, far=far, side=side):
                passed_chunk(far, k, side)
                return carry

            lax.fori_loop(first, last, passed, 0)

    if fast > 1:
        moved = full_ref.at[:, pl.ds(0, (fast - 1) * share)]
        pltpu.make_async_copy(moved, moved, side_recv.at[0]).wait()


def last_plane(a, slow):
    return jnp.where(2 * a < slow, slow - 1, 0)


def first_plane(a, slow):
    return jnp.where(2 * a < slow, 0, 1)


def gather_rest(dims, late_ref, chain_recv, side_recv):
    slow, fast, vcs, tiles, shared, size = dims
    share = (tiles - shared) // fast
    own_chunks, chunks = share // size, (share + shared) // size
    a = lax.div(lax.axis_index("vp"), fast)
    one = late_ref.at[pl.ds(0, size)]

    @pl.when((a == 0) | (a == slow - 1))
    def _():
        def arrived(k, carry):
            pltpu.make_async_copy(one, one, chain_recv.at[last_plane(a, slow), k]).wait()
            return carry

        lax.fori_loop(own_chunks, chunks, arrived, 0)

    if fast > 1:
        moved = late_ref.at[pl.ds(0, (fast - 1) * share)]
        pltpu.make_async_copy(moved, moved, side_recv.at[1]).wait()


def gather_sends(dims, full_ref, late_ref, pieces, piece_send, up_send, down_send, side_send):
    slow, fast, vcs, tiles, shared, size = dims
    share = (tiles - shared) // fast
    chunks = (share + shared) // size
    group = fast * vcs
    a = lax.div(lax.axis_index("vp"), fast)
    one = late_ref.at[pl.ds(0, size)]
    if fast > 1:
        moved = full_ref.at[:, pl.ds(0, (fast - 1) * share)]
        pltpu.make_async_copy(moved, moved, side_send.at[0]).wait()
        moved = late_ref.at[pl.ds(0, (fast - 1) * share)]
        pltpu.make_async_copy(moved, moved, side_send.at[1]).wait()
    sent = pieces.at[pl.ds(0, group - 1)]
    pltpu.make_async_copy(sent, sent, piece_send).wait()

    for far in range(slow):
        def sent_chunk(k, carry, far=far):
            @pl.when((a - far >= 0) & (a < slow - 1))
            def _():
                pltpu.make_async_copy(one, one, up_send.at[a - far, k]).wait()

            @pl.when((a + far < slow) & (a > 0))
            def _():
                pltpu.make_async_copy(one, one, down_send.at[a + far, k]).wait()

            return carry

        lax.fori_loop(0, chunks, sent_chunk, 0)


def sort_slots(count, pairs_ref, table):
    slots = pairs_ref.shape[1]
    ab_row = pairs_ref[0:1, :]
    rows = lax.broadcasted_iota(jnp.int32, (slots, slots), 0)
    lanes = lax.broadcasted_iota(jnp.int32, (slots, slots), 1)

    def as_column(row):
        return jnp.sum(jnp.where(rows == lanes, row, 0), axis=1, keepdims=True)

    slot_row = lax.broadcasted_iota(jnp.int32, (1, slots), 1)
    key_row = jnp.where(slot_row < count, ab_row, AB_TILES) * slots + slot_row
    key_col = as_column(key_row)
    rank_col = jnp.sum((key_row < key_col).astype(jnp.int32), axis=1, keepdims=True)
    chosen = rank_col == lanes

    def in_order(column):
        return jnp.sum(jnp.where(chosen, column, 0), axis=0, keepdims=True)

    table[...] = jnp.zeros_like(table)
    table[0:1, :] = in_order(rows[:, 0:1])
    table[1:2, :] = in_order(as_column(pairs_ref[1:2, :]))
    key_sorted = in_order(key_col)
    same = jnp.any((rank_col + 1 == lanes) & (lax.div(key_col, slots) == lax.div(key_sorted, slots)),
                   axis=0, keepdims=True)
    table[2:3, :] = same.astype(jnp.int32)
    table[3:4, :] = jnp.sum((key_col < (lanes + 1) * slots).astype(jnp.int32), axis=0, keepdims=True)


def multiply(load, plane, planes, row, rows, batch, smem, tiles, running, partial, plane_rows):
    slots, width = tiles.shape[0], tiles.shape[1]
    out_rows = partial.shape[2]
    height = planes * rows

    def step(j, total):
        base = j * batch
        products = []
        for n in range(batch):
            left = load(smem[1, base + n])
            products.append(jnp.dot(left.reshape(height, width), tiles[smem[0, base + n]],
                                    preferred_element_type=jnp.float32))
        for n in range(batch):
            total = total * smem[2, base + n].astype(jnp.float32) + products[n]
            running[base + n, :height] = total
        return total

    lax.fori_loop(0, slots // batch, step, jnp.zeros((height, width), jnp.float32))
    count = height // out_rows
    target = pl.ds(plane * (plane_rows // out_rows) + row // out_rows, count)
    for ab in range(AB_TILES):
        end = smem[3, ab]
        start = smem[3, ab - 1] if ab else 0
        some = jnp.minimum(end - start, 1).astype(jnp.float32)
        total = running[jnp.maximum(end - 1, 0), :height] * some
        partial[target, ab] = total.reshape(count, out_rows, width)


def ladder_kernel(dims, batch, parts, count_ref, pairs_ref, amp_ref, tiles_hbm, out_ref,
                  full, late_rows, pieces, tiles, running, partial, near, sums, far, table, smem,
                  piece_send, piece_recv, up_send, down_send, chain_recv, side_send, side_recv,
                  tile_sem, table_sem, near_send, near_recv, far_send, far_recv):
    slow, fast, vcs = dims[:3]
    plane_rows = full.shape[2]
    out_rows = partial.shape[2]
    width = tiles.shape[2]
    per_plane = plane_rows // out_rows
    outer = vcs // PAIR
    part = AB_TILES // parts
    vp = lax.axis_index("vp")
    c = lax.axis_index("vc")
    y, core = lax.div(c, PAIR), lax.rem(c, PAIR)
    late = last_plane(lax.div(vp, fast), slow)
    early = first_plane(lax.div(vp, fast), slow)

    def meanwhile():
        pltpu.make_async_copy(tiles_hbm, tiles, tile_sem).start()
        sort_slots(count_ref[0], pairs_ref, table)
        pltpu.make_async_copy(table, smem, table_sem).start()

    def window(h):
        return pl.ds(h * part, part)

    def near_copy(target, h):
        i = lax.div(target, PAIR)
        return pltpu.make_async_remote_copy(
            src_ref=partial.at[target, window(h)], dst_ref=near.at[i, window(h)],
            send_sem=near_send.at[i, h], recv_sem=near_recv.at[i, h],
            device_id=(vp, y * PAIR + 1 - core), device_id_type=MESH)

    def far_copy(i, h):
        return pltpu.make_async_remote_copy(
            src_ref=sums.at[i, window(h)], dst_ref=far.at[y, window(h)],
            send_sem=far_send.at[i, h], recv_sem=far_recv.at[y, h],
            device_id=(vp, i * PAIR + core), device_id_type=MESH)

    def to_core(target):
        @pl.when(lax.rem(target, PAIR) != core)
        def _():
            for h in range(parts):
                near_copy(target, h).start()

    def to_chip(target):
        i = lax.div(target, PAIR)

        @pl.when((lax.rem(target, PAIR) == core) & (i != y))
        def _():
            for h in range(parts):
                near_copy(target, h).wait_recv()
                sums[i, window(h)] = partial[target, window(h)] + near[i, window(h)]
                far_copy(i, h).start()

    def multiply_early():
        rows = running.shape[1]
        if rows >= (slow - 1) * plane_rows:
            multiply(lambda tile: full[:, tile], early, slow - 1, 0, plane_rows,
                     batch, smem, tiles, running, partial, plane_rows)
            return
        for p in range(slow - 1):
            for row in range(0, plane_rows, rows):
                multiply(lambda tile, p=p, row=row: full[p, tile, pl.ds(row, rows)], early + p, 1, row, rows,
                         batch, smem, tiles, running, partial, plane_rows)

    def multiply_late():
        rows = min(running.shape[1], plane_rows)
        for row in range(0, plane_rows, rows):
            multiply(lambda tile, row=row: late_rows[tile, pl.ds(row, rows)], late, 1, row, rows,
                     batch, smem, tiles, running, partial, plane_rows)

    gather(dims, amp_ref, full, late_rows, pieces, piece_send, piece_recv,
           up_send, down_send, chain_recv, side_send, side_recv, meanwhile)
    pltpu.make_async_copy(tiles_hbm, tiles, tile_sem).wait()
    pltpu.make_async_copy(table, smem, table_sem).wait()

    early_targets = [early * per_plane + n for n in range((slow - 1) * per_plane)]
    late_targets = [late * per_plane + n for n in range(per_plane)]
    multiply_early()
    for target in early_targets:
        to_core(target)
    gather_rest(dims, late_rows, chain_recv, side_recv)
    for target in early_targets:
        to_chip(target)
    multiply_late()
    for target in late_targets:
        to_core(target)
    for target in late_targets:
        to_chip(target)

    for h in range(parts):
        near_copy(c, h).wait_recv()
        total = partial[c, window(h)] + near[y, window(h)]
        for step in range(1, outer):
            source = lax.rem(y + step, outer)
            arrived = far.at[source, window(h)]
            pltpu.make_async_copy(arrived, arrived, far_recv.at[source, h]).wait()
            total = total + far[source, window(h)]
        for n in range(part):
            at = (h * part + n) * width
            out_ref[:, at:at + width] = total[n].astype(out_ref.dtype)

    for i in range(outer):
        for h in range(parts):
            near_copy(i * PAIR + 1 - core, h).wait_send()

            @pl.when(i != y)
            def _(i=i, h=h):
                far_copy(i, h).wait_send()

    gather_sends(dims, full, late_rows, pieces, piece_send, up_send, down_send, side_send)


def per_device(n_vp, n_vc, amplitudes, pair_tiles, slot_pairs, slot_count):
    own_rows, columns = amplitudes.shape
    slots, width, _ = pair_tiles.shape
    slow = SLOW if n_vp % SLOW == 0 else n_vp
    fast = n_vp // slow
    tiles = columns // width // n_vc
    rows = own_rows * n_vp * n_vc
    plane_rows = rows // slow
    shared = tiles // 5
    shared += (tiles - shared) % fast
    share = (tiles - shared) // fast
    size = largest_divisor(math.gcd(share, shared), 20)
    chunks = (share + shared) // size
    group = fast * n_vc
    in_vmem = pl.BlockSpec(memory_space=pltpu.VMEM)

    amp = amplitudes.reshape(own_rows, columns // width, width).transpose(1, 0, 2)
    out_rows = rows // n_vc
    early_rows = rows - plane_rows
    at_once = early_rows if early_rows <= 64 else min(plane_rows, 64)
    slots_batch = largest_divisor(slots, 16)
    outer = n_vc // PAIR
    parts = largest_divisor(AB_TILES, 4)
    block = (AB_TILES, out_rows, width)
    dma = pltpu.SemaphoreType.DMA
    in_smem = pl.BlockSpec(memory_space=pltpu.SMEM)
    return pl.pallas_call(
        functools.partial(
            ladder_kernel, (slow, fast, n_vc, tiles, shared, size), slots_batch, parts),
        out_shape=jax.ShapeDtypeStruct((out_rows, AB_TILES * width), jnp.bfloat16),
        in_specs=[in_smem, in_vmem, in_vmem, pl.BlockSpec(memory_space=pl.ANY)],
        out_specs=in_vmem,
        scratch_shapes=[
            pltpu.VMEM((slow - 1, tiles, plane_rows, width), amplitudes.dtype),
            pltpu.VMEM((tiles, plane_rows, width), amplitudes.dtype),
            pltpu.VMEM((group, share + shared, own_rows, width), amplitudes.dtype),
            pltpu.VMEM(pair_tiles.shape, pair_tiles.dtype),
            pltpu.VMEM((slots, at_once, width), jnp.float32),
            pltpu.VMEM((n_vc,) + block, jnp.float32),
            pltpu.VMEM((outer,) + block, jnp.float32),
            pltpu.VMEM((outer,) + block, jnp.float32),
            pltpu.VMEM((outer,) + block, jnp.float32),
            pltpu.VMEM((8, slots), jnp.int32),
            pltpu.SMEM((8, slots), jnp.int32),
            dma, dma((chunks,)),
            dma((slow, chunks)), dma((slow, chunks)), dma((slow, chunks)),
            dma((2,)), dma((2,)), dma, dma,
            dma((outer, parts)), dma((outer, parts)), dma((outer, parts)), dma((outer, parts)),
        ],
        compiler_params=pltpu.CompilerParams(
            collective_id=0, has_side_effects=True, vmem_limit_bytes=VMEM),
        name="ladder",
    )(slot_count, slot_pairs.T, amp, pair_tiles)


def solution(mesh):
    in_specs = (
        P(("vp", "vc"), None),
        P(("vp", "vc"), None, None),
        P(("vp", "vc"), None),
        P(("vp", "vc")),
    )
    return jax.shard_map(
        functools.partial(per_device, mesh.shape["vp"], mesh.shape["vc"]),
        mesh=mesh, in_specs=in_specs, out_specs=P("vc", "vp"), check_vma=False)
```

```python
import functools

import jax
import jax.numpy as jnp
from jax import lax
from jax.experimental import pallas as pl
from jax.experimental.pallas import tpu as pltpu
from jax.sharding import PartitionSpec as P

AB_TILES = 16
SLOW = 4
PAIR = 2
VMEM = 60 * 1024 * 1024
MESH = pl.DeviceIdType.MESH


def largest_divisor(value, limit):
    return max(d for d in range(1, limit + 1) if value % d == 0)


def gather(dims, amp_ref, full_ref, late_ref, pieces, piece_send, piece_recv,
           up_send, down_send, chain_recv, side_send, side_recv, meanwhile):
    slow, fast, vcs, tiles, shared, size = dims
    share = (tiles - shared) // fast
    held = share + shared
    height = amp_ref.shape[1]
    unit = tiles * vcs // amp_ref.shape[0]
    own_chunks, chunks = share // size, held // size
    group = fast * vcs
    vp = lax.axis_index("vp")
    c = lax.axis_index("vc")
    a, b = lax.div(vp, fast), lax.rem(vp, fast)
    me = b * vcs + c

    def in_plane(step):
        other = lax.rem(me + step, group)
        return lax.div(other, vcs), lax.rem(other, vcs)

    def plane_id(ob, oc):
        return (a * fast + ob, oc)

    def tile_at(ob, k):
        return jnp.where(k < own_chunks, ob * share + k * size, fast * share + (k - own_chunks) * size)

    barrier = pltpu.get_barrier_semaphore()

    def greet(step, carry):
        ob, oc = in_plane(step)
        pl.semaphore_signal(barrier, inc=1, device_id=plane_id(ob, oc), device_id_type=MESH)
        return carry

    lax.fori_loop(1, group, greet, 0)

    @pl.when(a > 0)
    def _():
        pl.semaphore_signal(barrier, inc=1, device_id=(vp - fast, c), device_id_type=MESH)

    @pl.when(a < slow - 1)
    def _():
        pl.semaphore_signal(barrier, inc=1, device_id=(vp + fast, c), device_id_type=MESH)

    edges = (a > 0).astype(jnp.int32) + (a < slow - 1).astype(jnp.int32)
    pl.semaphore_wait(barrier, group - 1 + edges)

    def send_pieces(k, carry):
        def one(step, carry):
            ob, oc = in_plane(step)
            pltpu.make_async_remote_copy(
                src_ref=amp_ref.at[pl.ds(lax.div(oc * tiles + tile_at(ob, k), unit), size // unit)],
                dst_ref=pieces.at[me, pl.ds(k * (size // unit), size // unit)],
                send_sem=piece_send, recv_sem=piece_recv.at[k],
                device_id=plane_id(ob, oc), device_id_type=MESH).start()
            return carry
        return lax.fori_loop(1, group, one, carry)

    ahead = min(4, chunks)
    lax.fori_loop(0, ahead, send_pieces, 0)
    pieces[me, :share // unit] = amp_ref[pl.ds(lax.div(c * tiles + b * share, unit), share // unit)]
    if shared:
        pieces[me, share // unit:] = amp_ref[pl.ds(lax.div(c * tiles + fast * share, unit), shared // unit)]

    block = unit * height
    to = lax.broadcasted_iota(jnp.int32, (block, block), 0)
    at = lax.broadcasted_iota(jnp.int32, (block, block), 1)
    own_rows = height // unit
    source, tile, r = lax.div(lax.rem(to, height), own_rows), lax.div(to, height), lax.rem(to, own_rows)
    order = (at == source * height + tile * own_rows + r).astype(jnp.float32).astype(amp_ref.dtype)

    def start_copy(plane, k, from_a, to_a, send_sem, recv_sem, device):
        window = pl.ds(tile_at(b, k), size)
        from_late, to_late = plane == last_plane(from_a, slow), plane == last_plane(to_a, slow)

        def place(is_late, at_a):
            return late_ref.at[window] if is_late else full_ref.at[plane - first_plane(at_a, slow), window]

        for source in (False, True):
            for target in (False, True):
                @pl.when((from_late == source) & (to_late == target))
                def _(source=source, target=target):
                    pltpu.make_async_remote_copy(
                        src_ref=place(source, from_a), dst_ref=place(target, to_a),
                        send_sem=send_sem, recv_sem=recv_sem,
                        device_id=device, device_id_type=MESH).start()

    def up(plane, k):
        start_copy(plane, k, a, a + 1, up_send.at[plane, k], chain_recv.at[plane, k], (vp + fast, c))

    def down(plane, k):
        start_copy(plane, k, a, a - 1, down_send.at[plane, k], chain_recv.at[plane, k], (vp - fast, c))

    def arrived(plane, k):
        one = late_ref.at[pl.ds(0, size)]
        pltpu.make_async_copy(one, one, chain_recv.at[plane, k]).wait()

    def sideways(plane, k):
        window = pl.ds(tile_at(b, k), size)
        is_late = plane == last_plane(a, slow)

        def one(step, carry):
            ob = lax.rem(b + step, fast)

            @pl.when(is_late)
            def _():
                pltpu.make_async_remote_copy(
                    src_ref=late_ref.at[window], dst_ref=late_ref.at[window],
                    send_sem=side_send.at[1], recv_sem=side_recv.at[1],
                    device_id=plane_id(ob, c), device_id_type=MESH).start()

            @pl.when(jnp.logical_not(is_late))
            def _():
                place = full_ref.at[plane - first_plane(a, slow), window]
                pltpu.make_async_remote_copy(
                    src_ref=place, dst_ref=place,
                    send_sem=side_send.at[0], recv_sem=side_recv.at[0],
                    device_id=plane_id(ob, c), device_id_type=MESH).start()

            return carry

        lax.fori_loop(1, fast, one, 0)

    def own_chunk(k, side):
        landed = pieces.at[pl.ds(0, group - 1), pl.ds(k * (size // unit), size // unit)]
        pltpu.make_async_copy(landed, landed, piece_recv.at[k]).wait()
        for n in range(size // unit):
            for i in range(group // unit):
                mixed = pieces[pl.ds(i * unit, unit), k * (size // unit) + n].reshape(block, -1)
                sorted_rows = jnp.dot(order, mixed, preferred_element_type=jnp.float32).astype(amp_ref.dtype)
                full_ref[a - first_plane(a, slow), pl.ds(tile_at(b, k) + n * unit, unit),
                         pl.ds(i * height, height)] = sorted_rows.reshape(unit, height, -1)

        @pl.when(a > 0)
        def _():
            down(a, k)

        @pl.when(a < slow - 1)
        def _():
            up(a, k)

        if side:
            sideways(a, k)

        @pl.when(k + ahead < chunks)
        def _():
            send_pieces(k + ahead, 0)

    def passed_chunk(far, k, side):
        @pl.when(a - far >= 0)
        def _():
            arrived(a - far, k)

            @pl.when(a < slow - 1)
            def _():
                up(a - far, k)

            if side:
                sideways(a - far, k)

        @pl.when(a + far < slow)
        def _():
            arrived(a + far, k)

            @pl.when(a > 0)
            def _():
                down(a + far, k)

            if side:
                sideways(a + far, k)

    for first, last, side in ((0, own_chunks, True), (own_chunks, chunks, False)):
        if first == last:
            continue

        def own(k, carry, side=side):
            own_chunk(k, side)
            return carry

        lax.fori_loop(first, last, own, 0)
        if first == 0:
            meanwhile()
        for far in range(1, slow if side else slow - 1):
            def passed(k, carry, far=far, side=side):
                passed_chunk(far, k, side)
                return carry

            lax.fori_loop(first, last, passed, 0)

    if fast > 1:
        moved = full_ref.at[:, pl.ds(0, (fast - 1) * share)]
        pltpu.make_async_copy(moved, moved, side_recv.at[0]).wait()


def last_plane(a, slow):
    return jnp.where(2 * a < slow, slow - 1, 0)


def first_plane(a, slow):
    return jnp.where(2 * a < slow, 0, 1)


def gather_rest(dims, late_ref, chain_recv, side_recv):
    slow, fast, vcs, tiles, shared, size = dims
    share = (tiles - shared) // fast
    own_chunks, chunks = share // size, (share + shared) // size
    a = lax.div(lax.axis_index("vp"), fast)
    one = late_ref.at[pl.ds(0, size)]

    @pl.when((a == 0) | (a == slow - 1))
    def _():
        def arrived(k, carry):
            pltpu.make_async_copy(one, one, chain_recv.at[last_plane(a, slow), k]).wait()
            return carry

        lax.fori_loop(own_chunks, chunks, arrived, 0)

    if fast > 1:
        moved = late_ref.at[pl.ds(0, (fast - 1) * share)]
        pltpu.make_async_copy(moved, moved, side_recv.at[1]).wait()


def gather_sends(dims, full_ref, late_ref, pieces, piece_send, up_send, down_send, side_send):
    slow, fast, vcs, tiles, shared, size = dims
    share = (tiles - shared) // fast
    chunks = (share + shared) // size
    group = fast * vcs
    a = lax.div(lax.axis_index("vp"), fast)
    one = late_ref.at[pl.ds(0, size)]
    if fast > 1:
        moved = full_ref.at[:, pl.ds(0, (fast - 1) * share)]
        pltpu.make_async_copy(moved, moved, side_send.at[0]).wait()
        moved = late_ref.at[pl.ds(0, (fast - 1) * share)]
        pltpu.make_async_copy(moved, moved, side_send.at[1]).wait()
    sent = pieces.at[pl.ds(0, group - 1)]
    pltpu.make_async_copy(sent, sent, piece_send).wait()

    for far in range(slow):
        def sent_chunk(k, carry, far=far):
            @pl.when((a - far >= 0) & (a < slow - 1))
            def _():
                pltpu.make_async_copy(one, one, up_send.at[a - far, k]).wait()

            @pl.when((a + far < slow) & (a > 0))
            def _():
                pltpu.make_async_copy(one, one, down_send.at[a + far, k]).wait()

            return carry

        lax.fori_loop(0, chunks, sent_chunk, 0)


def sort_slots(count, pairs_ref, table):
    slots = pairs_ref.shape[1]
    ab_row = pairs_ref[0:1, :]
    rows = lax.broadcasted_iota(jnp.int32, (slots, slots), 0)
    lanes = lax.broadcasted_iota(jnp.int32, (slots, slots), 1)

    def as_column(row):
        return jnp.sum(jnp.where(rows == lanes, row, 0), axis=1, keepdims=True)

    slot_row = lax.broadcasted_iota(jnp.int32, (1, slots), 1)
    key_row = jnp.where(slot_row < count, ab_row, AB_TILES) * slots + slot_row
    key_col = as_column(key_row)
    rank_col = jnp.sum((key_row < key_col).astype(jnp.int32), axis=1, keepdims=True)
    chosen = rank_col == lanes

    def in_order(column):
        return jnp.sum(jnp.where(chosen, column, 0), axis=0, keepdims=True)

    table[...] = jnp.zeros_like(table)
    table[0:1, :] = in_order(rows[:, 0:1])
    table[1:2, :] = in_order(as_column(pairs_ref[1:2, :]))
    key_sorted = in_order(key_col)
    same = jnp.any((rank_col + 1 == lanes) & (lax.div(key_col, slots) == lax.div(key_sorted, slots)),
                   axis=0, keepdims=True)
    table[2:3, :] = same.astype(jnp.int32)
    table[3:4, :] = jnp.sum((key_col < (lanes + 1) * slots).astype(jnp.int32), axis=0, keepdims=True)


def multiply(load, plane, planes, row, rows, batch, smem, tiles, running, partial, plane_rows):
    slots, width = tiles.shape[0], tiles.shape[1]
    out_rows = partial.shape[2]
    height = planes * rows

    def step(j, total):
        base = j * batch
        products = []
        for n in range(batch):
            left = load(smem[1, base + n])
            products.append(jnp.dot(left.reshape(height, width), tiles[smem[0, base + n]],
                                    preferred_element_type=jnp.float32))
        for n in range(batch):
            total = total * smem[2, base + n].astype(jnp.float32) + products[n]
            running[base + n, :height] = total
        return total

    lax.fori_loop(0, slots // batch, step, jnp.zeros((height, width), jnp.float32))
    count = height // out_rows
    target = pl.ds(plane * (plane_rows // out_rows) + row // out_rows, count)
    for ab in range(AB_TILES):
        end = smem[3, ab]
        start = smem[3, ab - 1] if ab else 0
        some = jnp.minimum(end - start, 1).astype(jnp.float32)
        total = running[jnp.maximum(end - 1, 0), :height] * some
        partial[target, ab] = total.reshape(count, out_rows, width)


def ladder_kernel(dims, batch, parts, count_ref, pairs_ref, amp_ref, tiles_hbm, out_ref,
                  full, late_rows, pieces, tiles, running, partial, near, sums, far, table, smem,
                  piece_send, piece_recv, up_send, down_send, chain_recv, side_send, side_recv,
                  tile_sem, table_sem, near_send, near_recv, far_send, far_recv):
    slow, fast, vcs = dims[:3]
    plane_rows = full.shape[2]
    out_rows = partial.shape[2]
    width = tiles.shape[2]
    per_plane = plane_rows // out_rows
    outer = vcs // PAIR
    part = AB_TILES // parts
    vp = lax.axis_index("vp")
    c = lax.axis_index("vc")
    y, core = lax.div(c, PAIR), lax.rem(c, PAIR)
    late = last_plane(lax.div(vp, fast), slow)
    early = first_plane(lax.div(vp, fast), slow)

    def meanwhile():
        pltpu.make_async_copy(tiles_hbm, tiles, tile_sem).start()
        sort_slots(count_ref[0], pairs_ref, table)
        pltpu.make_async_copy(table, smem, table_sem).start()

    def window(h):
        return pl.ds(h * part, part)

    def near_copy(target, h):
        i = lax.div(target, PAIR)
        return pltpu.make_async_remote_copy(
            src_ref=partial.at[target, window(h)], dst_ref=near.at[i, window(h)],
            send_sem=near_send.at[i, h], recv_sem=near_recv.at[i, h],
            device_id=(vp, y * PAIR + 1 - core), device_id_type=MESH)

    def far_copy(i, h):
        return pltpu.make_async_remote_copy(
            src_ref=sums.at[i, window(h)], dst_ref=far.at[y, window(h)],
            send_sem=far_send.at[i, h], recv_sem=far_recv.at[y, h],
            device_id=(vp, i * PAIR + core), device_id_type=MESH)

    def to_core(target):
        @pl.when(lax.rem(target, PAIR) != core)
        def _():
            for h in range(parts):
                near_copy(target, h).start()

    def to_chip(target):
        i = lax.div(target, PAIR)

        @pl.when((lax.rem(target, PAIR) == core) & (i != y))
        def _():
            for h in range(parts):
                near_copy(target, h).wait_recv()
                sums[i, window(h)] = partial[target, window(h)] + near[i, window(h)]
                far_copy(i, h).start()

    def multiply_early():
        rows = running.shape[1]
        if rows >= (slow - 1) * plane_rows:
            multiply(lambda tile: full[:, tile], early, slow - 1, 0, plane_rows,
                     batch, smem, tiles, running, partial, plane_rows)
            return
        for p in range(slow - 1):
            for row in range(0, plane_rows, rows):
                multiply(lambda tile, p=p, row=row: full[p, tile, pl.ds(row, rows)], early + p, 1, row, rows,
                         batch, smem, tiles, running, partial, plane_rows)

    def multiply_late():
        rows = min(running.shape[1], plane_rows)
        for row in range(0, plane_rows, rows):
            multiply(lambda tile, row=row: late_rows[tile, pl.ds(row, rows)], late, 1, row, rows,
                     batch, smem, tiles, running, partial, plane_rows)

    gather(dims, amp_ref, full, late_rows, pieces, piece_send, piece_recv,
           up_send, down_send, chain_recv, side_send, side_recv, meanwhile)
    pltpu.make_async_copy(tiles_hbm, tiles, tile_sem).wait()
    pltpu.make_async_copy(table, smem, table_sem).wait()

    early_targets = [early * per_plane + n for n in range((slow - 1) * per_plane)]
    late_targets = [late * per_plane + n for n in range(per_plane)]
    multiply_early()
    for target in early_targets:
        to_core(target)
    gather_rest(dims, late_rows, chain_recv, side_recv)
    for target in early_targets:
        to_chip(target)
    multiply_late()
    for target in late_targets:
        to_core(target)
    for target in late_targets:
        to_chip(target)

    for h in range(parts):
        near_copy(c, h).wait_recv()
        total = partial[c, window(h)] + near[y, window(h)]
        for step in range(1, outer):
            source = lax.rem(y + step, outer)
            arrived = far.at[source, window(h)]
            pltpu.make_async_copy(arrived, arrived, far_recv.at[source, h]).wait()
            total = total + far[source, window(h)]
        for n in range(part):
            at = (h * part + n) * width
            out_ref[:, at:at + width] = total[n].astype(out_ref.dtype)

    for i in range(outer):
        for h in range(parts):
            near_copy(i * PAIR + 1 - core, h).wait_send()

            @pl.when(i != y)
            def _(i=i, h=h):
                far_copy(i, h).wait_send()

    gather_sends(dims, full, late_rows, pieces, piece_send, up_send, down_send, side_send)


def per_device(n_vp, n_vc, amplitudes, pair_tiles, slot_pairs, slot_count):
    own_rows, columns = amplitudes.shape
    slots, width, _ = pair_tiles.shape
    slow = SLOW if n_vp % SLOW == 0 else n_vp
    fast = n_vp // slow
    tiles = columns // width // n_vc
    rows = own_rows * n_vp * n_vc
    plane_rows = rows // slow
    unit = 16 // own_rows
    share = (tiles - tiles // 5) // fast // unit * unit
    shared = tiles - fast * share
    size = unit
    chunks = (share + shared) // size
    group = fast * n_vc
    in_vmem = pl.BlockSpec(memory_space=pltpu.VMEM)

    amp = amplitudes.reshape(own_rows, columns // width, width).transpose(1, 0, 2)
    amp = amp.reshape(-1, unit * own_rows, width)
    out_rows = rows // n_vc
    early_rows = rows - plane_rows
    at_once = early_rows if early_rows <= 64 else min(plane_rows, 64)
    slots_batch = largest_divisor(slots, 16)
    outer = n_vc // PAIR
    parts = largest_divisor(AB_TILES, 4)
    block = (AB_TILES, out_rows, width)
    dma = pltpu.SemaphoreType.DMA
    in_smem = pl.BlockSpec(memory_space=pltpu.SMEM)
    return pl.pallas_call(
        functools.partial(
            ladder_kernel, (slow, fast, n_vc, tiles, shared, size), slots_batch, parts),
        out_shape=jax.ShapeDtypeStruct((out_rows, AB_TILES * width), jnp.bfloat16),
        in_specs=[in_smem, in_vmem, in_vmem, pl.BlockSpec(memory_space=pl.ANY)],
        out_specs=in_vmem,
        scratch_shapes=[
            pltpu.VMEM((slow - 1, tiles, plane_rows, width), amplitudes.dtype),
            pltpu.VMEM((tiles, plane_rows, width), amplitudes.dtype),
            pltpu.VMEM((group, (share + shared) // unit, unit * own_rows, width), amplitudes.dtype),
            pltpu.VMEM(pair_tiles.shape, pair_tiles.dtype),
            pltpu.VMEM((slots, at_once, width), jnp.float32),
            pltpu.VMEM((n_vc,) + block, jnp.float32),
            pltpu.VMEM((outer,) + block, jnp.float32),
            pltpu.VMEM((outer,) + block, jnp.float32),
            pltpu.VMEM((outer,) + block, jnp.float32),
            pltpu.VMEM((8, slots), jnp.int32),
            pltpu.SMEM((8, slots), jnp.int32),
            dma, dma((chunks,)),
            dma((slow, chunks)), dma((slow, chunks)), dma((slow, chunks)),
            dma((2,)), dma((2,)), dma, dma,
            dma((outer, parts)), dma((outer, parts)), dma((outer, parts)), dma((outer, parts)),
        ],
        compiler_params=pltpu.CompilerParams(
            collective_id=0, has_side_effects=True, vmem_limit_bytes=VMEM),
        name="ladder",
    )(slot_count, slot_pairs.T, amp, pair_tiles)


def solution(mesh):
    in_specs = (
        P(("vp", "vc"), None),
        P(("vp", "vc"), None, None),
        P(("vp", "vc"), None),
        P(("vp", "vc")),
    )
    return jax.shard_map(
        functools.partial(per_device, mesh.shape["vp"], mesh.shape["vc"]),
        mesh=mesh, in_specs=in_specs, out_specs=P("vc", "vp"), check_vma=False)
```

```python
import functools
import math

import jax
import jax.numpy as jnp
from jax import lax
from jax.experimental import pallas as pl
from jax.experimental.pallas import tpu as pltpu
from jax.sharding import PartitionSpec as P

AB_TILES = 16
SLOW = 4
PAIR = 2
VMEM = 60 * 1024 * 1024
MESH = pl.DeviceIdType.MESH


def largest_divisor(value, limit):
    return max(d for d in range(1, limit + 1) if value % d == 0)


def gather(dims, amp_ref, full_ref, late_ref, pieces, piece_send, piece_recv,
           up_send, down_send, chain_recv, side_send, side_recv, meanwhile):
    slow, fast, vcs, tiles, shared, size = dims
    share = (tiles - shared) // fast
    held = share + shared
    height = amp_ref.shape[1]
    unit = tiles * vcs // amp_ref.shape[0]
    own_chunks, chunks = share // size, held // size
    group = fast * vcs
    vp = lax.axis_index("vp")
    c = lax.axis_index("vc")
    a, b = lax.div(vp, fast), lax.rem(vp, fast)
    me = b * vcs + c

    def in_plane(step):
        other = lax.rem(me + step, group)
        return lax.div(other, vcs), lax.rem(other, vcs)

    def plane_id(ob, oc):
        return (a * fast + ob, oc)

    def tile_at(ob, k):
        return jnp.where(k < own_chunks, ob * share + k * size, fast * share + (k - own_chunks) * size)

    barrier = pltpu.get_barrier_semaphore()

    def greet(step, carry):
        ob, oc = in_plane(step)
        pl.semaphore_signal(barrier, inc=1, device_id=plane_id(ob, oc), device_id_type=MESH)
        return carry

    lax.fori_loop(1, group, greet, 0)

    @pl.when(a > 0)
    def _():
        pl.semaphore_signal(barrier, inc=1, device_id=(vp - fast, c), device_id_type=MESH)

    @pl.when(a < slow - 1)
    def _():
        pl.semaphore_signal(barrier, inc=1, device_id=(vp + fast, c), device_id_type=MESH)

    edges = (a > 0).astype(jnp.int32) + (a < slow - 1).astype(jnp.int32)
    pl.semaphore_wait(barrier, group - 1 + edges)

    def send_pieces(k, carry):
        def one(step, carry):
            ob, oc = in_plane(step)
            pltpu.make_async_remote_copy(
                src_ref=amp_ref.at[pl.ds(lax.div(oc * tiles + tile_at(ob, k), unit), size // unit)],
                dst_ref=pieces.at[me, pl.ds(k * (size // unit), size // unit)],
                send_sem=piece_send, recv_sem=piece_recv.at[k],
                device_id=plane_id(ob, oc), device_id_type=MESH).start()
            return carry
        return lax.fori_loop(1, group, one, carry)

    ahead = min(2, chunks)
    lax.fori_loop(0, ahead, send_pieces, 0)
    pieces[me, :share // unit] = amp_ref[pl.ds(lax.div(c * tiles + b * share, unit), share // unit)]
    if shared:
        pieces[me, share // unit:] = amp_ref[pl.ds(lax.div(c * tiles + fast * share, unit), shared // unit)]

    block = unit * height
    to = lax.broadcasted_iota(jnp.int32, (block, block), 0)
    at = lax.broadcasted_iota(jnp.int32, (block, block), 1)
    own_rows = height // unit
    source, tile, r = lax.div(lax.rem(to, height), own_rows), lax.div(to, height), lax.rem(to, own_rows)
    order = (at == source * height + tile * own_rows + r).astype(jnp.float32).astype(amp_ref.dtype)

    def start_copy(plane, k, from_a, to_a, send_sem, recv_sem, device):
        window = pl.ds(tile_at(b, k), size)
        from_late, to_late = plane == last_plane(from_a, slow), plane == last_plane(to_a, slow)

        def place(is_late, at_a):
            return late_ref.at[window] if is_late else full_ref.at[plane - first_plane(at_a, slow), window]

        for source in (False, True):
            for target in (False, True):
                @pl.when((from_late == source) & (to_late == target))
                def _(source=source, target=target):
                    pltpu.make_async_remote_copy(
                        src_ref=place(source, from_a), dst_ref=place(target, to_a),
                        send_sem=send_sem, recv_sem=recv_sem,
                        device_id=device, device_id_type=MESH).start()

    def up(plane, k):
        start_copy(plane, k, a, a + 1, up_send.at[plane, k], chain_recv.at[plane, k], (vp + fast, c))

    def down(plane, k):
        start_copy(plane, k, a, a - 1, down_send.at[plane, k], chain_recv.at[plane, k], (vp - fast, c))

    def arrived(plane, k):
        one = late_ref.at[pl.ds(0, size)]
        pltpu.make_async_copy(one, one, chain_recv.at[plane, k]).wait()

    def sideways(plane, k):
        window = pl.ds(tile_at(b, k), size)
        is_late = plane == last_plane(a, slow)

        def one(step, carry):
            ob = lax.rem(b + step, fast)

            @pl.when(is_late)
            def _():
                pltpu.make_async_remote_copy(
                    src_ref=late_ref.at[window], dst_ref=late_ref.at[window],
                    send_sem=side_send.at[1], recv_sem=side_recv.at[1],
                    device_id=plane_id(ob, c), device_id_type=MESH).start()

            @pl.when(jnp.logical_not(is_late))
            def _():
                place = full_ref.at[plane - first_plane(a, slow), window]
                pltpu.make_async_remote_copy(
                    src_ref=place, dst_ref=place,
                    send_sem=side_send.at[0], recv_sem=side_recv.at[0],
                    device_id=plane_id(ob, c), device_id_type=MESH).start()

            return carry

        lax.fori_loop(1, fast, one, 0)

    def own_chunk(k, side):
        landed = pieces.at[pl.ds(0, group - 1), pl.ds(k * (size // unit), size // unit)]
        pltpu.make_async_copy(landed, landed, piece_recv.at[k]).wait()
        for n in range(size // unit):
            for i in range(group // unit):
                mixed = pieces[pl.ds(i * unit, unit), k * (size // unit) + n].reshape(block, -1)
                sorted_rows = jnp.dot(order, mixed, preferred_element_type=jnp.float32).astype(amp_ref.dtype)
                full_ref[a - first_plane(a, slow), pl.ds(tile_at(b, k) + n * unit, unit),
                         pl.ds(i * height, height)] = sorted_rows.reshape(unit, height, -1)

        @pl.when(a > 0)
        def _():
            down(a, k)

        @pl.when(a < slow - 1)
        def _():
            up(a, k)

        if side:
            sideways(a, k)

        @pl.when(k + ahead < chunks)
        def _():
            send_pieces(k + ahead, 0)

    def passed_chunk(far, k, side):
        @pl.when(a - far >= 0)
        def _():
            arrived(a - far, k)

            @pl.when(a < slow - 1)
            def _():
                up(a - far, k)

            if side:
                sideways(a - far, k)

        @pl.when(a + far < slow)
        def _():
            arrived(a + far, k)

            @pl.when(a > 0)
            def _():
                down(a + far, k)

            if side:
                sideways(a + far, k)

    for first, last, side in ((0, own_chunks, True), (own_chunks, chunks, False)):
        if first == last:
            continue

        def own(k, carry, side=side):
            own_chunk(k, side)
            return carry

        lax.fori_loop(first, last, own, 0)
        if first == 0:
            meanwhile()
        for far in range(1, slow if side else slow - 1):
            def passed(k, carry, far=far, side=side):
                passed_chunk(far, k, side)
                return carry

            lax.fori_loop(first, last, passed, 0)

    if fast > 1:
        moved = full_ref.at[:, pl.ds(0, (fast - 1) * share)]
        pltpu.make_async_copy(moved, moved, side_recv.at[0]).wait()


def last_plane(a, slow):
    return jnp.where(2 * a < slow, slow - 1, 0)


def first_plane(a, slow):
    return jnp.where(2 * a < slow, 0, 1)


def gather_rest(dims, late_ref, chain_recv, side_recv):
    slow, fast, vcs, tiles, shared, size = dims
    share = (tiles - shared) // fast
    own_chunks, chunks = share // size, (share + shared) // size
    a = lax.div(lax.axis_index("vp"), fast)
    one = late_ref.at[pl.ds(0, size)]

    @pl.when((a == 0) | (a == slow - 1))
    def _():
        def arrived(k, carry):
            pltpu.make_async_copy(one, one, chain_recv.at[last_plane(a, slow), k]).wait()
            return carry

        lax.fori_loop(own_chunks, chunks, arrived, 0)

    if fast > 1:
        moved = late_ref.at[pl.ds(0, (fast - 1) * share)]
        pltpu.make_async_copy(moved, moved, side_recv.at[1]).wait()


def gather_sends(dims, full_ref, late_ref, pieces, piece_send, up_send, down_send, side_send):
    slow, fast, vcs, tiles, shared, size = dims
    share = (tiles - shared) // fast
    chunks = (share + shared) // size
    group = fast * vcs
    a = lax.div(lax.axis_index("vp"), fast)
    one = late_ref.at[pl.ds(0, size)]
    if fast > 1:
        moved = full_ref.at[:, pl.ds(0, (fast - 1) * share)]
        pltpu.make_async_copy(moved, moved, side_send.at[0]).wait()
        moved = late_ref.at[pl.ds(0, (fast - 1) * share)]
        pltpu.make_async_copy(moved, moved, side_send.at[1]).wait()
    sent = pieces.at[pl.ds(0, group - 1)]
    pltpu.make_async_copy(sent, sent, piece_send).wait()

    for far in range(slow):
        def sent_chunk(k, carry, far=far):
            @pl.when((a - far >= 0) & (a < slow - 1))
            def _():
                pltpu.make_async_copy(one, one, up_send.at[a - far, k]).wait()

            @pl.when((a + far < slow) & (a > 0))
            def _():
                pltpu.make_async_copy(one, one, down_send.at[a + far, k]).wait()

            return carry

        lax.fori_loop(0, chunks, sent_chunk, 0)


def sort_slots(count, pairs_ref, table):
    slots = pairs_ref.shape[1]
    ab_row = pairs_ref[0:1, :]
    rows = lax.broadcasted_iota(jnp.int32, (slots, slots), 0)
    lanes = lax.broadcasted_iota(jnp.int32, (slots, slots), 1)

    def as_column(row):
        return jnp.sum(jnp.where(rows == lanes, row, 0), axis=1, keepdims=True)

    slot_row = lax.broadcasted_iota(jnp.int32, (1, slots), 1)
    key_row = jnp.where(slot_row < count, ab_row, AB_TILES) * slots + slot_row
    key_col = as_column(key_row)
    rank_col = jnp.sum((key_row < key_col).astype(jnp.int32), axis=1, keepdims=True)
    chosen = rank_col == lanes

    def in_order(column):
        return jnp.sum(jnp.where(chosen, column, 0), axis=0, keepdims=True)

    table[...] = jnp.zeros_like(table)
    table[0:1, :] = in_order(rows[:, 0:1])
    table[1:2, :] = in_order(as_column(pairs_ref[1:2, :]))
    key_sorted = in_order(key_col)
    same = jnp.any((rank_col + 1 == lanes) & (lax.div(key_col, slots) == lax.div(key_sorted, slots)),
                   axis=0, keepdims=True)
    table[2:3, :] = same.astype(jnp.int32)
    table[3:4, :] = jnp.sum((key_col < (lanes + 1) * slots).astype(jnp.int32), axis=0, keepdims=True)


def multiply(load, plane, planes, row, rows, batch, smem, tiles, running, partial, plane_rows):
    slots, width = tiles.shape[0], tiles.shape[1]
    out_rows = partial.shape[2]
    height = planes * rows

    def step(j, total):
        base = j * batch
        products = []
        for n in range(batch):
            left = load(smem[1, base + n])
            products.append(jnp.dot(left.reshape(height, width), tiles[smem[0, base + n]],
                                    preferred_element_type=jnp.float32))
        for n in range(batch):
            total = total * smem[2, base + n].astype(jnp.float32) + products[n]
            running[base + n, :height] = total
        return total

    lax.fori_loop(0, slots // batch, step, jnp.zeros((height, width), jnp.float32))
    count = height // out_rows
    target = pl.ds(plane * (plane_rows // out_rows) + row // out_rows, count)
    for ab in range(AB_TILES):
        end = smem[3, ab]
        start = smem[3, ab - 1] if ab else 0
        some = jnp.minimum(end - start, 1).astype(jnp.float32)
        total = running[jnp.maximum(end - 1, 0), :height] * some
        partial[target, ab] = total.reshape(count, out_rows, width)


def ladder_kernel(dims, batch, parts, count_ref, pairs_ref, amp_ref, tiles_hbm, out_ref,
                  full, late_rows, pieces, tiles, running, partial, near, sums, far, table, smem,
                  piece_send, piece_recv, up_send, down_send, chain_recv, side_send, side_recv,
                  tile_sem, table_sem, near_send, near_recv, far_send, far_recv):
    slow, fast, vcs = dims[:3]
    plane_rows = full.shape[2]
    out_rows = partial.shape[2]
    width = tiles.shape[2]
    per_plane = plane_rows // out_rows
    outer = vcs // PAIR
    part = AB_TILES // parts
    vp = lax.axis_index("vp")
    c = lax.axis_index("vc")
    y, core = lax.div(c, PAIR), lax.rem(c, PAIR)
    late = last_plane(lax.div(vp, fast), slow)
    early = first_plane(lax.div(vp, fast), slow)

    def meanwhile():
        pltpu.make_async_copy(tiles_hbm, tiles, tile_sem).start()
        sort_slots(count_ref[0], pairs_ref, table)
        pltpu.make_async_copy(table, smem, table_sem).start()

    def window(h):
        return pl.ds(h * part, part)

    def near_copy(target, h):
        i = lax.div(target, PAIR)
        return pltpu.make_async_remote_copy(
            src_ref=partial.at[target, window(h)], dst_ref=near.at[i, window(h)],
            send_sem=near_send.at[i, h], recv_sem=near_recv.at[i, h],
            device_id=(vp, y * PAIR + 1 - core), device_id_type=MESH)

    def far_copy(i, h):
        return pltpu.make_async_remote_copy(
            src_ref=sums.at[i, window(h)], dst_ref=far.at[y, window(h)],
            send_sem=far_send.at[i, h], recv_sem=far_recv.at[y, h],
            device_id=(vp, i * PAIR + core), device_id_type=MESH)

    def to_core(target):
        @pl.when(lax.rem(target, PAIR) != core)
        def _():
            for h in range(parts):
                near_copy(target, h).start()

    def to_chip(target):
        i = lax.div(target, PAIR)

        @pl.when((lax.rem(target, PAIR) == core) & (i != y))
        def _():
            for h in range(parts):
                near_copy(target, h).wait_recv()
                sums[i, window(h)] = partial[target, window(h)] + near[i, window(h)]
                far_copy(i, h).start()

    def multiply_early():
        rows = running.shape[1]
        if rows >= (slow - 1) * plane_rows:
            multiply(lambda tile: full[:, tile], early, slow - 1, 0, plane_rows,
                     batch, smem, tiles, running, partial, plane_rows)
            return
        for p in range(slow - 1):
            for row in range(0, plane_rows, rows):
                multiply(lambda tile, p=p, row=row: full[p, tile, pl.ds(row, rows)], early + p, 1, row, rows,
                         batch, smem, tiles, running, partial, plane_rows)

    def multiply_late():
        rows = min(running.shape[1], plane_rows)
        for row in range(0, plane_rows, rows):
            multiply(lambda tile, row=row: late_rows[tile, pl.ds(row, rows)], late, 1, row, rows,
                     batch, smem, tiles, running, partial, plane_rows)

    gather(dims, amp_ref, full, late_rows, pieces, piece_send, piece_recv,
           up_send, down_send, chain_recv, side_send, side_recv, meanwhile)
    pltpu.make_async_copy(tiles_hbm, tiles, tile_sem).wait()
    pltpu.make_async_copy(table, smem, table_sem).wait()

    early_targets = [early * per_plane + n for n in range((slow - 1) * per_plane)]
    late_targets = [late * per_plane + n for n in range(per_plane)]
    multiply_early()
    for target in early_targets:
        to_core(target)
    gather_rest(dims, late_rows, chain_recv, side_recv)
    for target in early_targets:
        to_chip(target)
    multiply_late()
    for target in late_targets:
        to_core(target)
    for target in late_targets:
        to_chip(target)

    for h in range(parts):
        near_copy(c, h).wait_recv()
        total = partial[c, window(h)] + near[y, window(h)]
        for step in range(1, outer):
            source = lax.rem(y + step, outer)
            arrived = far.at[source, window(h)]
            pltpu.make_async_copy(arrived, arrived, far_recv.at[source, h]).wait()
            total = total + far[source, window(h)]
        for n in range(part):
            at = (h * part + n) * width
            out_ref[:, at:at + width] = total[n].astype(out_ref.dtype)

    for i in range(outer):
        for h in range(parts):
            near_copy(i * PAIR + 1 - core, h).wait_send()

            @pl.when(i != y)
            def _(i=i, h=h):
                far_copy(i, h).wait_send()

    gather_sends(dims, full, late_rows, pieces, piece_send, up_send, down_send, side_send)


def per_device(n_vp, n_vc, amplitudes, pair_tiles, slot_pairs, slot_count):
    own_rows, columns = amplitudes.shape
    slots, width, _ = pair_tiles.shape
    slow = SLOW if n_vp % SLOW == 0 else n_vp
    fast = n_vp // slow
    tiles = columns // width // n_vc
    rows = own_rows * n_vp * n_vc
    plane_rows = rows // slow
    unit = 16 // own_rows
    share = (tiles - tiles // 5) // fast // unit * unit
    shared = tiles - fast * share
    size = math.gcd(share, shared)
    chunks = (share + shared) // size
    group = fast * n_vc
    in_vmem = pl.BlockSpec(memory_space=pltpu.VMEM)

    amp = amplitudes.reshape(own_rows, columns // width, width).transpose(1, 0, 2)
    amp = amp.reshape(-1, unit * own_rows, width)
    out_rows = rows // n_vc
    early_rows = rows - plane_rows
    at_once = early_rows if early_rows <= 64 else min(plane_rows, 64)
    slots_batch = largest_divisor(slots, 16)
    outer = n_vc // PAIR
    parts = largest_divisor(AB_TILES, 4)
    block = (AB_TILES, out_rows, width)
    dma = pltpu.SemaphoreType.DMA
    in_smem = pl.BlockSpec(memory_space=pltpu.SMEM)
    return pl.pallas_call(
        functools.partial(
            ladder_kernel, (slow, fast, n_vc, tiles, shared, size), slots_batch, parts),
        out_shape=jax.ShapeDtypeStruct((out_rows, AB_TILES * width), jnp.bfloat16),
        in_specs=[in_smem, in_vmem, in_vmem, pl.BlockSpec(memory_space=pl.ANY)],
        out_specs=in_vmem,
        scratch_shapes=[
            pltpu.VMEM((slow - 1, tiles, plane_rows, width), amplitudes.dtype),
            pltpu.VMEM((tiles, plane_rows, width), amplitudes.dtype),
            pltpu.VMEM((group, (share + shared) // unit, unit * own_rows, width), amplitudes.dtype),
            pltpu.VMEM(pair_tiles.shape, pair_tiles.dtype),
            pltpu.VMEM((slots, at_once, width), jnp.float32),
            pltpu.VMEM((n_vc,) + block, jnp.float32),
            pltpu.VMEM((outer,) + block, jnp.float32),
            pltpu.VMEM((outer,) + block, jnp.float32),
            pltpu.VMEM((outer,) + block, jnp.float32),
            pltpu.VMEM((8, slots), jnp.int32),
            pltpu.SMEM((8, slots), jnp.int32),
            dma, dma((chunks,)),
            dma((slow, chunks)), dma((slow, chunks)), dma((slow, chunks)),
            dma((2,)), dma((2,)), dma, dma,
            dma((outer, parts)), dma((outer, parts)), dma((outer, parts)), dma((outer, parts)),
        ],
        compiler_params=pltpu.CompilerParams(
            collective_id=0, has_side_effects=True, vmem_limit_bytes=VMEM),
        name="ladder",
    )(slot_count, slot_pairs.T, amp, pair_tiles)


def solution(mesh):
    in_specs = (
        P(("vp", "vc"), None),
        P(("vp", "vc"), None, None),
        P(("vp", "vc"), None),
        P(("vp", "vc")),
    )
    return jax.shard_map(
        functools.partial(per_device, mesh.shape["vp"], mesh.shape["vc"]),
        mesh=mesh, in_specs=in_specs, out_specs=P("vc", "vp"), check_vma=False)
```

```python
import functools
import math

import jax
import jax.numpy as jnp
from jax import lax
from jax.experimental import pallas as pl
from jax.experimental.pallas import tpu as pltpu
from jax.sharding import PartitionSpec as P

AB_TILES = 16
SLOW = 4
PAIR = 2
VMEM = 60 * 1024 * 1024
MESH = pl.DeviceIdType.MESH


def largest_divisor(value, limit):
    return max(d for d in range(1, limit + 1) if value % d == 0)


def gather(dims, amp_ref, full_ref, late_ref, pieces, piece_send, piece_recv,
           up_send, down_send, chain_recv, side_send, side_recv, meanwhile):
    slow, fast, vcs, tiles, shared, size = dims
    share = (tiles - shared) // fast
    held = share + shared
    height = amp_ref.shape[1]
    unit = tiles * vcs // amp_ref.shape[0]
    own_chunks, chunks = share // size, held // size
    group = fast * vcs
    vp = lax.axis_index("vp")
    c = lax.axis_index("vc")
    a, b = lax.div(vp, fast), lax.rem(vp, fast)
    me = b * vcs + c

    def in_plane(step):
        other = lax.rem(me + step, group)
        return lax.div(other, vcs), lax.rem(other, vcs)

    def plane_id(ob, oc):
        return (a * fast + ob, oc)

    def tile_at(ob, k):
        return jnp.where(k < own_chunks, ob * share + k * size, fast * share + (k - own_chunks) * size)

    barrier = pltpu.get_barrier_semaphore()

    def greet(step, carry):
        ob, oc = in_plane(step)
        pl.semaphore_signal(barrier, inc=1, device_id=plane_id(ob, oc), device_id_type=MESH)
        return carry

    lax.fori_loop(1, group, greet, 0)

    @pl.when(a > 0)
    def _():
        pl.semaphore_signal(barrier, inc=1, device_id=(vp - fast, c), device_id_type=MESH)

    @pl.when(a < slow - 1)
    def _():
        pl.semaphore_signal(barrier, inc=1, device_id=(vp + fast, c), device_id_type=MESH)

    edges = (a > 0).astype(jnp.int32) + (a < slow - 1).astype(jnp.int32)
    pl.semaphore_wait(barrier, group - 1 + edges)

    def send_pieces(k, carry):
        def one(step, carry):
            ob, oc = in_plane(step)
            pltpu.make_async_remote_copy(
                src_ref=amp_ref.at[pl.ds(lax.div(oc * tiles + tile_at(ob, k), unit), size // unit)],
                dst_ref=pieces.at[me, pl.ds(k * (size // unit), size // unit)],
                send_sem=piece_send, recv_sem=piece_recv.at[k],
                device_id=plane_id(ob, oc), device_id_type=MESH).start()
            return carry
        return lax.fori_loop(1, group, one, carry)

    ahead = min(2, chunks)
    lax.fori_loop(0, ahead, send_pieces, 0)
    pieces[me, :share // unit] = amp_ref[pl.ds(lax.div(c * tiles + b * share, unit), share // unit)]
    if shared:
        pieces[me, share // unit:] = amp_ref[pl.ds(lax.div(c * tiles + fast * share, unit), shared // unit)]

    block = unit * height
    to = lax.broadcasted_iota(jnp.int32, (block, block), 0)
    at = lax.broadcasted_iota(jnp.int32, (block, block), 1)
    own_rows = height // unit
    source, tile, r = lax.div(lax.rem(to, height), own_rows), lax.div(to, height), lax.rem(to, own_rows)
    order = (at == source * height + tile * own_rows + r).astype(jnp.float32).astype(amp_ref.dtype)

    def start_copy(plane, k, from_a, to_a, send_sem, recv_sem, device):
        window = pl.ds(tile_at(b, k), size)
        from_late, to_late = plane == last_plane(from_a, slow), plane == last_plane(to_a, slow)

        def place(is_late, at_a):
            return late_ref.at[window] if is_late else full_ref.at[plane - first_plane(at_a, slow), window]

        for source in (False, True):
            for target in (False, True):
                @pl.when((from_late == source) & (to_late == target))
                def _(source=source, target=target):
                    pltpu.make_async_remote_copy(
                        src_ref=place(source, from_a), dst_ref=place(target, to_a),
                        send_sem=send_sem, recv_sem=recv_sem,
                        device_id=device, device_id_type=MESH).start()

    def up(plane, k):
        start_copy(plane, k, a, a + 1, up_send.at[plane, k], chain_recv.at[plane, k], (vp + fast, c))

    def down(plane, k):
        start_copy(plane, k, a, a - 1, down_send.at[plane, k], chain_recv.at[plane, k], (vp - fast, c))

    def arrived(plane, k):
        one = late_ref.at[pl.ds(0, size)]
        pltpu.make_async_copy(one, one, chain_recv.at[plane, k]).wait()

    def sideways(plane, k):
        window = pl.ds(tile_at(b, k), size)
        is_late = plane == last_plane(a, slow)

        def one(step, carry):
            ob = lax.rem(b + step, fast)

            @pl.when(is_late)
            def _():
                pltpu.make_async_remote_copy(
                    src_ref=late_ref.at[window], dst_ref=late_ref.at[window],
                    send_sem=side_send.at[1], recv_sem=side_recv.at[1],
                    device_id=plane_id(ob, c), device_id_type=MESH).start()

            @pl.when(jnp.logical_not(is_late))
            def _():
                place = full_ref.at[plane - first_plane(a, slow), window]
                pltpu.make_async_remote_copy(
                    src_ref=place, dst_ref=place,
                    send_sem=side_send.at[0], recv_sem=side_recv.at[0],
                    device_id=plane_id(ob, c), device_id_type=MESH).start()

            return carry

        lax.fori_loop(1, fast, one, 0)

    def own_chunk(k, side):
        landed = pieces.at[pl.ds(0, group - 1), pl.ds(k * (size // unit), size // unit)]
        pltpu.make_async_copy(landed, landed, piece_recv.at[k]).wait()
        for n in range(size // unit):
            for i in range(group // unit):
                mixed = pieces[pl.ds(i * unit, unit), k * (size // unit) + n].reshape(block, -1)
                sorted_rows = jnp.dot(order, mixed, preferred_element_type=jnp.float32).astype(amp_ref.dtype)
                full_ref[a - first_plane(a, slow), pl.ds(tile_at(b, k) + n * unit, unit),
                         pl.ds(i * height, height)] = sorted_rows.reshape(unit, height, -1)

        @pl.when(a > 0)
        def _():
            down(a, k)

        @pl.when(a < slow - 1)
        def _():
            up(a, k)

        if side:
            sideways(a, k)

        @pl.when(k + ahead < chunks)
        def _():
            send_pieces(k + ahead, 0)

    def passed_chunk(far, k, side):
        @pl.when(a - far >= 0)
        def _():
            arrived(a - far, k)

            @pl.when(a < slow - 1)
            def _():
                up(a - far, k)

            if side:
                sideways(a - far, k)

        @pl.when(a + far < slow)
        def _():
            arrived(a + far, k)

            @pl.when(a > 0)
            def _():
                down(a + far, k)

            if side:
                sideways(a + far, k)

    phases = [(first, last, side) for first, last, side in
              ((0, own_chunks, True), (own_chunks, chunks, False)) if first < last]
    for first, last, side in phases:
        def own(k, carry, side=side):
            own_chunk(k, side)
            return carry

        lax.fori_loop(first, last, own, 0)
    meanwhile()
    for first, last, side in phases:
        for far in range(1, slow if side else slow - 1):
            def passed(k, carry, far=far, side=side):
                passed_chunk(far, k, side)
                return carry

            lax.fori_loop(first, last, passed, 0)

    if fast > 1:
        moved = full_ref.at[:, pl.ds(0, (fast - 1) * share)]
        pltpu.make_async_copy(moved, moved, side_recv.at[0]).wait()


def last_plane(a, slow):
    return jnp.where(2 * a < slow, slow - 1, 0)


def first_plane(a, slow):
    return jnp.where(2 * a < slow, 0, 1)


def gather_rest(dims, late_ref, chain_recv, side_recv):
    slow, fast, vcs, tiles, shared, size = dims
    share = (tiles - shared) // fast
    own_chunks, chunks = share // size, (share + shared) // size
    a = lax.div(lax.axis_index("vp"), fast)
    one = late_ref.at[pl.ds(0, size)]

    @pl.when((a == 0) | (a == slow - 1))
    def _():
        def arrived(k, carry):
            pltpu.make_async_copy(one, one, chain_recv.at[last_plane(a, slow), k]).wait()
            return carry

        lax.fori_loop(own_chunks, chunks, arrived, 0)

    if fast > 1:
        moved = late_ref.at[pl.ds(0, (fast - 1) * share)]
        pltpu.make_async_copy(moved, moved, side_recv.at[1]).wait()


def gather_sends(dims, full_ref, late_ref, pieces, piece_send, up_send, down_send, side_send):
    slow, fast, vcs, tiles, shared, size = dims
    share = (tiles - shared) // fast
    chunks = (share + shared) // size
    group = fast * vcs
    a = lax.div(lax.axis_index("vp"), fast)
    one = late_ref.at[pl.ds(0, size)]
    if fast > 1:
        moved = full_ref.at[:, pl.ds(0, (fast - 1) * share)]
        pltpu.make_async_copy(moved, moved, side_send.at[0]).wait()
        moved = late_ref.at[pl.ds(0, (fast - 1) * share)]
        pltpu.make_async_copy(moved, moved, side_send.at[1]).wait()
    sent = pieces.at[pl.ds(0, group - 1)]
    pltpu.make_async_copy(sent, sent, piece_send).wait()

    for far in range(slow):
        def sent_chunk(k, carry, far=far):
            @pl.when((a - far >= 0) & (a < slow - 1))
            def _():
                pltpu.make_async_copy(one, one, up_send.at[a - far, k]).wait()

            @pl.when((a + far < slow) & (a > 0))
            def _():
                pltpu.make_async_copy(one, one, down_send.at[a + far, k]).wait()

            return carry

        lax.fori_loop(0, chunks, sent_chunk, 0)


def sort_slots(count, pairs_ref, table):
    slots = pairs_ref.shape[1]
    ab_row = pairs_ref[0:1, :]
    rows = lax.broadcasted_iota(jnp.int32, (slots, slots), 0)
    lanes = lax.broadcasted_iota(jnp.int32, (slots, slots), 1)

    def as_column(row):
        return jnp.sum(jnp.where(rows == lanes, row, 0), axis=1, keepdims=True)

    slot_row = lax.broadcasted_iota(jnp.int32, (1, slots), 1)
    key_row = jnp.where(slot_row < count, ab_row, AB_TILES) * slots + slot_row
    key_col = as_column(key_row)
    rank_col = jnp.sum((key_row < key_col).astype(jnp.int32), axis=1, keepdims=True)
    chosen = rank_col == lanes

    def in_order(column):
        return jnp.sum(jnp.where(chosen, column, 0), axis=0, keepdims=True)

    table[...] = jnp.zeros_like(table)
    table[0:1, :] = in_order(rows[:, 0:1])
    table[1:2, :] = in_order(as_column(pairs_ref[1:2, :]))
    key_sorted = in_order(key_col)
    same = jnp.any((rank_col + 1 == lanes) & (lax.div(key_col, slots) == lax.div(key_sorted, slots)),
                   axis=0, keepdims=True)
    table[2:3, :] = same.astype(jnp.int32)
    table[3:4, :] = jnp.sum((key_col < (lanes + 1) * slots).astype(jnp.int32), axis=0, keepdims=True)


def multiply(load, plane, planes, row, rows, batch, smem, tiles, running, partial, plane_rows):
    slots, width = tiles.shape[0], tiles.shape[1]
    out_rows = partial.shape[2]
    height = planes * rows

    def step(j, total):
        base = j * batch
        products = []
        for n in range(batch):
            left = load(smem[1, base + n])
            products.append(jnp.dot(left.reshape(height, width), tiles[smem[0, base + n]],
                                    preferred_element_type=jnp.float32))
        for n in range(batch):
            total = total * smem[2, base + n].astype(jnp.float32) + products[n]
            running[base + n, :height] = total
        return total

    lax.fori_loop(0, slots // batch, step, jnp.zeros((height, width), jnp.float32))
    count = height // out_rows
    target = pl.ds(plane * (plane_rows // out_rows) + row // out_rows, count)
    for ab in range(AB_TILES):
        end = smem[3, ab]
        start = smem[3, ab - 1] if ab else 0
        some = jnp.minimum(end - start, 1).astype(jnp.float32)
        total = running[jnp.maximum(end - 1, 0), :height] * some
        partial[target, ab] = total.reshape(count, out_rows, width)


def ladder_kernel(dims, batch, parts, count_ref, pairs_ref, amp_ref, tiles_hbm, out_ref,
                  full, late_rows, pieces, tiles, running, partial, near, sums, far, table, smem,
                  piece_send, piece_recv, up_send, down_send, chain_recv, side_send, side_recv,
                  tile_sem, table_sem, near_send, near_recv, far_send, far_recv):
    slow, fast, vcs = dims[:3]
    plane_rows = full.shape[2]
    out_rows = partial.shape[2]
    width = tiles.shape[2]
    per_plane = plane_rows // out_rows
    outer = vcs // PAIR
    part = AB_TILES // parts
    vp = lax.axis_index("vp")
    c = lax.axis_index("vc")
    y, core = lax.div(c, PAIR), lax.rem(c, PAIR)
    late = last_plane(lax.div(vp, fast), slow)
    early = first_plane(lax.div(vp, fast), slow)

    def meanwhile():
        pltpu.make_async_copy(tiles_hbm, tiles, tile_sem).start()
        sort_slots(count_ref[0], pairs_ref, table)
        pltpu.make_async_copy(table, smem, table_sem).start()

    def window(h):
        return pl.ds(h * part, part)

    def near_copy(target, h):
        i = lax.div(target, PAIR)
        return pltpu.make_async_remote_copy(
            src_ref=partial.at[target, window(h)], dst_ref=near.at[i, window(h)],
            send_sem=near_send.at[i, h], recv_sem=near_recv.at[i, h],
            device_id=(vp, y * PAIR + 1 - core), device_id_type=MESH)

    def far_copy(i, h):
        return pltpu.make_async_remote_copy(
            src_ref=sums.at[i, window(h)], dst_ref=far.at[y, window(h)],
            send_sem=far_send.at[i, h], recv_sem=far_recv.at[y, h],
            device_id=(vp, i * PAIR + core), device_id_type=MESH)

    def to_core(target):
        @pl.when(lax.rem(target, PAIR) != core)
        def _():
            for h in range(parts):
                near_copy(target, h).start()

    def to_chip(target):
        i = lax.div(target, PAIR)

        @pl.when((lax.rem(target, PAIR) == core) & (i != y))
        def _():
            for h in range(parts):
                near_copy(target, h).wait_recv()
                sums[i, window(h)] = partial[target, window(h)] + near[i, window(h)]
                far_copy(i, h).start()

    def multiply_early():
        rows = running.shape[1]
        if rows >= (slow - 1) * plane_rows:
            multiply(lambda tile: full[:, tile], early, slow - 1, 0, plane_rows,
                     batch, smem, tiles, running, partial, plane_rows)
            return
        for p in range(slow - 1):
            for row in range(0, plane_rows, rows):
                multiply(lambda tile, p=p, row=row: full[p, tile, pl.ds(row, rows)], early + p, 1, row, rows,
                         batch, smem, tiles, running, partial, plane_rows)

    def multiply_late():
        rows = min(running.shape[1], plane_rows)
        for row in range(0, plane_rows, rows):
            multiply(lambda tile, row=row: late_rows[tile, pl.ds(row, rows)], late, 1, row, rows,
                     batch, smem, tiles, running, partial, plane_rows)

    gather(dims, amp_ref, full, late_rows, pieces, piece_send, piece_recv,
           up_send, down_send, chain_recv, side_send, side_recv, meanwhile)
    pltpu.make_async_copy(tiles_hbm, tiles, tile_sem).wait()
    pltpu.make_async_copy(table, smem, table_sem).wait()

    early_targets = [early * per_plane + n for n in range((slow - 1) * per_plane)]
    late_targets = [late * per_plane + n for n in range(per_plane)]
    multiply_early()
    for target in early_targets:
        to_core(target)
    gather_rest(dims, late_rows, chain_recv, side_recv)
    for target in early_targets:
        to_chip(target)
    multiply_late()
    for target in late_targets:
        to_core(target)
    for target in late_targets:
        to_chip(target)

    for h in range(parts):
        near_copy(c, h).wait_recv()
        total = partial[c, window(h)] + near[y, window(h)]
        for step in range(1, outer):
            source = lax.rem(y + step, outer)
            arrived = far.at[source, window(h)]
            pltpu.make_async_copy(arrived, arrived, far_recv.at[source, h]).wait()
            total = total + far[source, window(h)]
        for n in range(part):
            at = (h * part + n) * width
            out_ref[:, at:at + width] = total[n].astype(out_ref.dtype)

    for i in range(outer):
        for h in range(parts):
            near_copy(i * PAIR + 1 - core, h).wait_send()

            @pl.when(i != y)
            def _(i=i, h=h):
                far_copy(i, h).wait_send()

    gather_sends(dims, full, late_rows, pieces, piece_send, up_send, down_send, side_send)


def per_device(n_vp, n_vc, amplitudes, pair_tiles, slot_pairs, slot_count):
    own_rows, columns = amplitudes.shape
    slots, width, _ = pair_tiles.shape
    slow = SLOW if n_vp % SLOW == 0 else n_vp
    fast = n_vp // slow
    tiles = columns // width // n_vc
    rows = own_rows * n_vp * n_vc
    plane_rows = rows // slow
    unit = 16 // own_rows
    share = (tiles - tiles // 5) // fast // unit * unit
    shared = tiles - fast * share
    size = math.gcd(share, shared)
    chunks = (share + shared) // size
    group = fast * n_vc
    in_vmem = pl.BlockSpec(memory_space=pltpu.VMEM)

    amp = amplitudes.reshape(own_rows, columns // width, width).transpose(1, 0, 2)
    amp = amp.reshape(-1, unit * own_rows, width)
    out_rows = rows // n_vc
    early_rows = rows - plane_rows
    at_once = early_rows if early_rows <= 64 else min(plane_rows, 64)
    slots_batch = largest_divisor(slots, 16)
    outer = n_vc // PAIR
    parts = largest_divisor(AB_TILES, 4)
    block = (AB_TILES, out_rows, width)
    dma = pltpu.SemaphoreType.DMA
    in_smem = pl.BlockSpec(memory_space=pltpu.SMEM)
    return pl.pallas_call(
        functools.partial(
            ladder_kernel, (slow, fast, n_vc, tiles, shared, size), slots_batch, parts),
        out_shape=jax.ShapeDtypeStruct((out_rows, AB_TILES * width), jnp.bfloat16),
        in_specs=[in_smem, in_vmem, in_vmem, pl.BlockSpec(memory_space=pl.ANY)],
        out_specs=in_vmem,
        scratch_shapes=[
            pltpu.VMEM((slow - 1, tiles, plane_rows, width), amplitudes.dtype),
            pltpu.VMEM((tiles, plane_rows, width), amplitudes.dtype),
            pltpu.VMEM((group, (share + shared) // unit, unit * own_rows, width), amplitudes.dtype),
            pltpu.VMEM(pair_tiles.shape, pair_tiles.dtype),
            pltpu.VMEM((slots, at_once, width), jnp.float32),
            pltpu.VMEM((n_vc,) + block, jnp.float32),
            pltpu.VMEM((outer,) + block, jnp.float32),
            pltpu.VMEM((outer,) + block, jnp.float32),
            pltpu.VMEM((outer,) + block, jnp.float32),
            pltpu.VMEM((8, slots), jnp.int32),
            pltpu.SMEM((8, slots), jnp.int32),
            dma, dma((chunks,)),
            dma((slow, chunks)), dma((slow, chunks)), dma((slow, chunks)),
            dma((2,)), dma((2,)), dma, dma,
            dma((outer, parts)), dma((outer, parts)), dma((outer, parts)), dma((outer, parts)),
        ],
        compiler_params=pltpu.CompilerParams(
            collective_id=0, has_side_effects=True, vmem_limit_bytes=VMEM),
        name="ladder",
    )(slot_count, slot_pairs.T, amp, pair_tiles)


def solution(mesh):
    in_specs = (
        P(("vp", "vc"), None),
        P(("vp", "vc"), None, None),
        P(("vp", "vc"), None),
        P(("vp", "vc")),
    )
    return jax.shard_map(
        functools.partial(per_device, mesh.shape["vp"], mesh.shape["vc"]),
        mesh=mesh, in_specs=in_specs, out_specs=P("vc", "vp"), check_vma=False)
```

```python
import functools
import math

import jax
import jax.numpy as jnp
from jax import lax
from jax.experimental import pallas as pl
from jax.experimental.pallas import tpu as pltpu
from jax.sharding import PartitionSpec as P

AB_TILES = 16
SLOW = 4
PAIR = 2
VMEM = 60 * 1024 * 1024
MESH = pl.DeviceIdType.MESH


def largest_divisor(value, limit):
    return max(d for d in range(1, limit + 1) if value % d == 0)


def gather(dims, amp_ref, full_ref, late_ref, pieces, piece_send, piece_recv,
           up_send, down_send, chain_recv, side_send, side_recv, meanwhile):
    slow, fast, vcs, tiles, shared, size = dims
    share = (tiles - shared) // fast
    held = share + shared
    height = amp_ref.shape[1]
    unit = tiles * vcs // amp_ref.shape[0]
    own_chunks, chunks = share // size, held // size
    group = fast * vcs
    vp = lax.axis_index("vp")
    c = lax.axis_index("vc")
    a, b = lax.div(vp, fast), lax.rem(vp, fast)
    me = b * vcs + c

    def in_plane(step):
        other = lax.rem(me + step, group)
        return lax.div(other, vcs), lax.rem(other, vcs)

    def plane_id(ob, oc):
        return (a * fast + ob, oc)

    def tile_at(ob, k):
        return jnp.where(k < own_chunks, ob * share + k * size, fast * share + (k - own_chunks) * size)

    barrier = pltpu.get_barrier_semaphore()

    def greet(step, carry):
        ob, oc = in_plane(step)
        pl.semaphore_signal(barrier, inc=1, device_id=plane_id(ob, oc), device_id_type=MESH)
        return carry

    lax.fori_loop(1, group, greet, 0)

    @pl.when(a > 0)
    def _():
        pl.semaphore_signal(barrier, inc=1, device_id=(vp - fast, c), device_id_type=MESH)

    @pl.when(a < slow - 1)
    def _():
        pl.semaphore_signal(barrier, inc=1, device_id=(vp + fast, c), device_id_type=MESH)

    edges = (a > 0).astype(jnp.int32) + (a < slow - 1).astype(jnp.int32)
    pl.semaphore_wait(barrier, group - 1 + edges)

    def send_pieces(k, carry):
        def one(step, carry):
            ob, oc = in_plane(step)
            pltpu.make_async_remote_copy(
                src_ref=amp_ref.at[pl.ds(lax.div(oc * tiles + tile_at(ob, k), unit), size // unit)],
                dst_ref=pieces.at[me, pl.ds(k * (size // unit), size // unit)],
                send_sem=piece_send, recv_sem=piece_recv.at[k],
                device_id=plane_id(ob, oc), device_id_type=MESH).start()
            return carry
        return lax.fori_loop(1, group, one, carry)

    ahead = min(2, chunks)
    lax.fori_loop(0, ahead, send_pieces, 0)
    pieces[me, :share // unit] = amp_ref[pl.ds(lax.div(c * tiles + b * share, unit), share // unit)]
    if shared:
        pieces[me, share // unit:] = amp_ref[pl.ds(lax.div(c * tiles + fast * share, unit), shared // unit)]

    block = unit * height
    to = lax.broadcasted_iota(jnp.int32, (block, block), 0)
    at = lax.broadcasted_iota(jnp.int32, (block, block), 1)
    own_rows = height // unit
    source, tile, r = lax.div(lax.rem(to, height), own_rows), lax.div(to, height), lax.rem(to, own_rows)
    order = (at == source * height + tile * own_rows + r).astype(jnp.float32).astype(amp_ref.dtype)

    def start_copy(plane, k, from_a, to_a, send_sem, recv_sem, device):
        window = pl.ds(tile_at(b, k), size)
        from_late, to_late = plane == last_plane(from_a, slow), plane == last_plane(to_a, slow)

        def place(is_late, at_a):
            return late_ref.at[window] if is_late else full_ref.at[plane - first_plane(at_a, slow), window]

        for source in (False, True):
            for target in (False, True):
                @pl.when((from_late == source) & (to_late == target))
                def _(source=source, target=target):
                    pltpu.make_async_remote_copy(
                        src_ref=place(source, from_a), dst_ref=place(target, to_a),
                        send_sem=send_sem, recv_sem=recv_sem,
                        device_id=device, device_id_type=MESH).start()

    def up(plane, k):
        start_copy(plane, k, a, a + 1, up_send.at[plane, k], chain_recv.at[plane, k], (vp + fast, c))

    def down(plane, k):
        start_copy(plane, k, a, a - 1, down_send.at[plane, k], chain_recv.at[plane, k], (vp - fast, c))

    def arrived(plane, k):
        one = late_ref.at[pl.ds(0, size)]
        pltpu.make_async_copy(one, one, chain_recv.at[plane, k]).wait()

    def sideways(plane, k):
        window = pl.ds(tile_at(b, k), size)
        is_late = plane == last_plane(a, slow)

        def one(step, carry):
            ob = lax.rem(b + step, fast)

            @pl.when(is_late)
            def _():
                pltpu.make_async_remote_copy(
                    src_ref=late_ref.at[window], dst_ref=late_ref.at[window],
                    send_sem=side_send.at[1], recv_sem=side_recv.at[1],
                    device_id=plane_id(ob, c), device_id_type=MESH).start()

            @pl.when(jnp.logical_not(is_late))
            def _():
                place = full_ref.at[plane - first_plane(a, slow), window]
                pltpu.make_async_remote_copy(
                    src_ref=place, dst_ref=place,
                    send_sem=side_send.at[0], recv_sem=side_recv.at[0],
                    device_id=plane_id(ob, c), device_id_type=MESH).start()

            return carry

        lax.fori_loop(1, fast, one, 0)

    def own_chunk(k, side):
        landed = pieces.at[pl.ds(0, group - 1), pl.ds(k * (size // unit), size // unit)]
        pltpu.make_async_copy(landed, landed, piece_recv.at[k]).wait()
        for n in range(size // unit):
            for i in range(group // unit):
                mixed = pieces[pl.ds(i * unit, unit), k * (size // unit) + n].reshape(block, -1)
                sorted_rows = jnp.dot(order, mixed, preferred_element_type=jnp.float32).astype(amp_ref.dtype)
                full_ref[a - first_plane(a, slow), pl.ds(tile_at(b, k) + n * unit, unit),
                         pl.ds(i * height, height)] = sorted_rows.reshape(unit, height, -1)

        @pl.when(a > 0)
        def _():
            down(a, k)

        @pl.when(a < slow - 1)
        def _():
            up(a, k)

        if side:
            sideways(a, k)

        @pl.when(k + ahead < chunks)
        def _():
            send_pieces(k + ahead, 0)

    def passed_chunk(far, k, side):
        @pl.when(a - far >= 0)
        def _():
            arrived(a - far, k)

            @pl.when(a < slow - 1)
            def _():
                up(a - far, k)

            if side:
                sideways(a - far, k)

        @pl.when(a + far < slow)
        def _():
            arrived(a + far, k)

            @pl.when(a > 0)
            def _():
                down(a + far, k)

            if side:
                sideways(a + far, k)

    phases = [(first, last, side) for first, last, side in
              ((0, own_chunks, True), (own_chunks, chunks, False)) if first < last]
    for first, last, side in phases:
        def own(k, carry, side=side):
            own_chunk(k, side)
            return carry

        lax.fori_loop(first, last, own, 0)
    meanwhile()
    for first, last, side in phases:
        for far in range(1, slow if side else slow - 1):
            def passed(k, carry, far=far, side=side):
                passed_chunk(far, k, side)
                return carry

            lax.fori_loop(first, last, passed, 0)

    if fast > 1:
        moved = full_ref.at[:, pl.ds(0, (fast - 1) * share)]
        pltpu.make_async_copy(moved, moved, side_recv.at[0]).wait()


def last_plane(a, slow):
    return jnp.where(2 * a < slow, slow - 1, 0)


def first_plane(a, slow):
    return jnp.where(2 * a < slow, 0, 1)


def gather_rest(dims, late_ref, chain_recv, side_recv):
    slow, fast, vcs, tiles, shared, size = dims
    share = (tiles - shared) // fast
    own_chunks, chunks = share // size, (share + shared) // size
    a = lax.div(lax.axis_index("vp"), fast)
    one = late_ref.at[pl.ds(0, size)]

    @pl.when((a == 0) | (a == slow - 1))
    def _():
        def arrived(k, carry):
            pltpu.make_async_copy(one, one, chain_recv.at[last_plane(a, slow), k]).wait()
            return carry

        lax.fori_loop(own_chunks, chunks, arrived, 0)

    if fast > 1:
        moved = late_ref.at[pl.ds(0, (fast - 1) * share)]
        pltpu.make_async_copy(moved, moved, side_recv.at[1]).wait()


def gather_sends(dims, full_ref, late_ref, pieces, piece_send, up_send, down_send, side_send):
    slow, fast, vcs, tiles, shared, size = dims
    share = (tiles - shared) // fast
    chunks = (share + shared) // size
    group = fast * vcs
    a = lax.div(lax.axis_index("vp"), fast)
    one = late_ref.at[pl.ds(0, size)]
    if fast > 1:
        moved = full_ref.at[:, pl.ds(0, (fast - 1) * share)]
        pltpu.make_async_copy(moved, moved, side_send.at[0]).wait()
        moved = late_ref.at[pl.ds(0, (fast - 1) * share)]
        pltpu.make_async_copy(moved, moved, side_send.at[1]).wait()
    sent = pieces.at[pl.ds(0, group - 1)]
    pltpu.make_async_copy(sent, sent, piece_send).wait()

    for far in range(slow):
        def sent_chunk(k, carry, far=far):
            @pl.when((a - far >= 0) & (a < slow - 1))
            def _():
                pltpu.make_async_copy(one, one, up_send.at[a - far, k]).wait()

            @pl.when((a + far < slow) & (a > 0))
            def _():
                pltpu.make_async_copy(one, one, down_send.at[a + far, k]).wait()

            return carry

        lax.fori_loop(0, chunks, sent_chunk, 0)


def sort_slots(count, pairs_ref, table):
    slots = pairs_ref.shape[1]
    ab_row = pairs_ref[0:1, :]
    rows = lax.broadcasted_iota(jnp.int32, (slots, slots), 0)
    lanes = lax.broadcasted_iota(jnp.int32, (slots, slots), 1)

    def as_column(row):
        return jnp.sum(jnp.where(rows == lanes, row, 0), axis=1, keepdims=True)

    slot_row = lax.broadcasted_iota(jnp.int32, (1, slots), 1)
    key_row = jnp.where(slot_row < count, ab_row, AB_TILES) * slots + slot_row
    key_col = as_column(key_row)
    rank_col = jnp.sum((key_row < key_col).astype(jnp.int32), axis=1, keepdims=True)
    chosen = rank_col == lanes

    def in_order(column):
        return jnp.sum(jnp.where(chosen, column, 0), axis=0, keepdims=True)

    table[...] = jnp.zeros_like(table)
    table[0:1, :] = in_order(rows[:, 0:1])
    table[1:2, :] = in_order(as_column(pairs_ref[1:2, :]))
    key_sorted = in_order(key_col)
    same = jnp.any((rank_col + 1 == lanes) & (lax.div(key_col, slots) == lax.div(key_sorted, slots)),
                   axis=0, keepdims=True)
    table[2:3, :] = same.astype(jnp.int32)
    table[3:4, :] = jnp.sum((key_col < (lanes + 1) * slots).astype(jnp.int32), axis=0, keepdims=True)


def multiply(load, plane, planes, row, rows, batch, smem, tiles, running, partial, plane_rows):
    slots, width = tiles.shape[0], tiles.shape[1]
    out_rows = partial.shape[2]
    height = planes * rows

    def step(j, total):
        base = j * batch
        products = []
        for n in range(batch):
            left = load(smem[1, base + n])
            products.append(jnp.dot(left.reshape(height, width), tiles[smem[0, base + n]],
                                    preferred_element_type=jnp.float32))
        for n in range(batch):
            total = total * smem[2, base + n].astype(jnp.float32) + products[n]
            running[base + n, :height] = total
        return total

    lax.fori_loop(0, slots // batch, step, jnp.zeros((height, width), jnp.float32))
    count = height // out_rows
    target = pl.ds(plane * (plane_rows // out_rows) + row // out_rows, count)
    for ab in range(AB_TILES):
        end = smem[3, ab]
        start = smem[3, ab - 1] if ab else 0
        some = jnp.minimum(end - start, 1).astype(jnp.float32)
        total = running[jnp.maximum(end - 1, 0), :height] * some
        partial[target, ab] = total.reshape(count, out_rows, width)


def ladder_kernel(dims, batch, parts, count_ref, pairs_ref, amp_ref, tiles_hbm, out_ref,
                  full, late_rows, pieces, tiles, running, partial, near, sums, far, table, smem,
                  piece_send, piece_recv, up_send, down_send, chain_recv, side_send, side_recv,
                  tile_sem, table_sem, near_send, near_recv, far_send, far_recv):
    slow, fast, vcs = dims[:3]
    plane_rows = full.shape[2]
    out_rows = partial.shape[2]
    width = tiles.shape[2]
    per_plane = plane_rows // out_rows
    outer = vcs // PAIR
    part = AB_TILES // parts
    vp = lax.axis_index("vp")
    c = lax.axis_index("vc")
    y, core = lax.div(c, PAIR), lax.rem(c, PAIR)
    late = last_plane(lax.div(vp, fast), slow)
    early = first_plane(lax.div(vp, fast), slow)

    def meanwhile():
        pltpu.make_async_copy(tiles_hbm, tiles, tile_sem).start()
        sort_slots(count_ref[0], pairs_ref, table)
        pltpu.make_async_copy(table, smem, table_sem).start()

    def window(h):
        return pl.ds(h * part, part)

    def near_copy(target, h):
        i = lax.div(target, PAIR)
        return pltpu.make_async_remote_copy(
            src_ref=partial.at[target, window(h)], dst_ref=near.at[i, window(h)],
            send_sem=near_send.at[i, h], recv_sem=near_recv.at[i, h],
            device_id=(vp, y * PAIR + 1 - core), device_id_type=MESH)

    def far_copy(i, h):
        return pltpu.make_async_remote_copy(
            src_ref=sums.at[i, window(h)], dst_ref=far.at[y, window(h)],
            send_sem=far_send.at[i, h], recv_sem=far_recv.at[y, h],
            device_id=(vp, i * PAIR + core), device_id_type=MESH)

    def to_core(target):
        @pl.when(lax.rem(target, PAIR) != core)
        def _():
            for h in range(parts):
                near_copy(target, h).start()

    def to_chip(target):
        i = lax.div(target, PAIR)

        @pl.when((lax.rem(target, PAIR) == core) & (i != y))
        def _():
            for h in range(parts):
                near_copy(target, h).wait_recv()
                sums[i, window(h)] = partial[target, window(h)] + near[i, window(h)]
                far_copy(i, h).start()

    def multiply_early():
        rows = running.shape[1]
        if rows >= (slow - 1) * plane_rows:
            multiply(lambda tile: full[:, tile], early, slow - 1, 0, plane_rows,
                     batch, smem, tiles, running, partial, plane_rows)
            return
        for p in range(slow - 1):
            for row in range(0, plane_rows, rows):
                multiply(lambda tile, p=p, row=row: full[p, tile, pl.ds(row, rows)], early + p, 1, row, rows,
                         batch, smem, tiles, running, partial, plane_rows)

    def multiply_late():
        rows = min(running.shape[1], plane_rows)
        for row in range(0, plane_rows, rows):
            multiply(lambda tile, row=row: late_rows[tile, pl.ds(row, rows)], late, 1, row, rows,
                     batch, smem, tiles, running, partial, plane_rows)

    gather(dims, amp_ref, full, late_rows, pieces, piece_send, piece_recv,
           up_send, down_send, chain_recv, side_send, side_recv, meanwhile)
    pltpu.make_async_copy(tiles_hbm, tiles, tile_sem).wait()
    pltpu.make_async_copy(table, smem, table_sem).wait()

    early_targets = [early * per_plane + n for n in range((slow - 1) * per_plane)]
    late_targets = [late * per_plane + n for n in range(per_plane)]
    multiply_early()
    for target in early_targets:
        to_core(target)
    gather_rest(dims, late_rows, chain_recv, side_recv)
    for target in early_targets:
        to_chip(target)
    multiply_late()
    for target in late_targets:
        to_core(target)
    for target in late_targets:
        to_chip(target)

    for h in range(parts):
        near_copy(c, h).wait_recv()
        total = partial[c, window(h)] + near[y, window(h)]
        for step in range(1, outer):
            source = lax.rem(y + step, outer)
            arrived = far.at[source, window(h)]
            pltpu.make_async_copy(arrived, arrived, far_recv.at[source, h]).wait()
            total = total + far[source, window(h)]
        for n in range(part):
            at = (h * part + n) * width
            out_ref[:, at:at + width] = total[n].astype(out_ref.dtype)

    for i in range(outer):
        for h in range(parts):
            near_copy(i * PAIR + 1 - core, h).wait_send()

            @pl.when(i != y)
            def _(i=i, h=h):
                far_copy(i, h).wait_send()

    gather_sends(dims, full, late_rows, pieces, piece_send, up_send, down_send, side_send)


def per_device(n_vp, n_vc, amplitudes, pair_tiles, slot_pairs, slot_count):
    own_rows, columns = amplitudes.shape
    slots, width, _ = pair_tiles.shape
    slow = SLOW if n_vp % SLOW == 0 else n_vp
    fast = n_vp // slow
    tiles = columns // width // n_vc
    rows = own_rows * n_vp * n_vc
    plane_rows = rows // slow
    unit = 16 // own_rows
    share = (tiles - tiles // 5) // fast // unit * unit
    shared = tiles - fast * share
    size = math.gcd(share, shared)
    chunks = (share + shared) // size
    group = fast * n_vc
    in_vmem = pl.BlockSpec(memory_space=pltpu.VMEM)

    amp = amplitudes.reshape(own_rows, columns // width, width).transpose(1, 0, 2)
    amp = amp.reshape(-1, unit * own_rows, width)
    out_rows = rows // n_vc
    early_rows = rows - plane_rows
    at_once = early_rows if early_rows <= 64 else min(plane_rows, 64)
    slots_batch = largest_divisor(slots, 16)
    outer = n_vc // PAIR
    parts = largest_divisor(AB_TILES, 2)
    block = (AB_TILES, out_rows, width)
    dma = pltpu.SemaphoreType.DMA
    in_smem = pl.BlockSpec(memory_space=pltpu.SMEM)
    return pl.pallas_call(
        functools.partial(
            ladder_kernel, (slow, fast, n_vc, tiles, shared, size), slots_batch, parts),
        out_shape=jax.ShapeDtypeStruct((out_rows, AB_TILES * width), jnp.bfloat16),
        in_specs=[in_smem, in_vmem, in_vmem, pl.BlockSpec(memory_space=pl.ANY)],
        out_specs=in_vmem,
        scratch_shapes=[
            pltpu.VMEM((slow - 1, tiles, plane_rows, width), amplitudes.dtype),
            pltpu.VMEM((tiles, plane_rows, width), amplitudes.dtype),
            pltpu.VMEM((group, (share + shared) // unit, unit * own_rows, width), amplitudes.dtype),
            pltpu.VMEM(pair_tiles.shape, pair_tiles.dtype),
            pltpu.VMEM((slots, at_once, width), jnp.float32),
            pltpu.VMEM((n_vc,) + block, jnp.float32),
            pltpu.VMEM((outer,) + block, jnp.float32),
            pltpu.VMEM((outer,) + block, jnp.float32),
            pltpu.VMEM((outer,) + block, jnp.float32),
            pltpu.VMEM((8, slots), jnp.int32),
            pltpu.SMEM((8, slots), jnp.int32),
            dma, dma((chunks,)),
            dma((slow, chunks)), dma((slow, chunks)), dma((slow, chunks)),
            dma((2,)), dma((2,)), dma, dma,
            dma((outer, parts)), dma((outer, parts)), dma((outer, parts)), dma((outer, parts)),
        ],
        compiler_params=pltpu.CompilerParams(
            collective_id=0, has_side_effects=True, vmem_limit_bytes=VMEM),
        name="ladder",
    )(slot_count, slot_pairs.T, amp, pair_tiles)


def solution(mesh):
    in_specs = (
        P(("vp", "vc"), None),
        P(("vp", "vc"), None, None),
        P(("vp", "vc"), None),
        P(("vp", "vc")),
    )
    return jax.shard_map(
        functools.partial(per_device, mesh.shape["vp"], mesh.shape["vc"]),
        mesh=mesh, in_specs=in_specs, out_specs=P("vc", "vp"), check_vma=False)
```
